512 devices in a mesh: src: 32 (over z, core), tgt: 16 (over y, x).
Axes of the slice: x: 4, y: 4, z: 16, core: 2. Of those that a mesh axis runs over, the one named last changes fastest.
Arguments:
- source_cells: bfloat16 [32768, 512], P('src'), may hold values from -6 to 6
- target_cells: bfloat16 [16384, 512], P('tgt'), may hold values from -6 to 6
- source_mass: float32 [32768], P('src'), may hold values from 0.25 to 4
- target_mass: float32 [16384], P('tgt'), may hold values from 0.25 to 4
- source_order: int32 [32768], P('src'), may hold values from 0 to 1023, as said below
- tile_list: int32 [32, 192], P('src', 'tgt'), may hold values from -1 to 15, as said below
- tile_count: int32 [32, 16], P('src', 'tgt'), may hold values from 4 to 12, as said below
Outputs:
- projected: bfloat16 [32768, 512], P(('src', 'tgt'))
- log_mass: float32 [32768], P(('src', 'tgt'))
The draws below stay inside these ranges and needn't reach their ends.
Inputs may be any that keep to these rules, and one draw needn't show every extreme that they name: `source_order`: each block of 1024 entries is a permutation of 0 to 1023. `tile_list`: the live entries of one list are distinct codes p * 4 + q of local block pairs, and every local source block and every local target block of the pair of shards occurs among them; entries past the count are -1. `tile_count`: counts vary from pair to pair of shards; some pair has 12.
All inputs are finite; a program needn't handle non-finite values.
Results may differ from the reference program's by a relative error of at most 0.009.
Values sent between devices are 32-bit elements; how exact they have to be, the bound alone decides.
A program may use at most 64 MiB of HBM per device.

```python
import math
import jax
import jax.numpy as jnp
from jax import lax

EMB = 512
BLK = 256
SDEV = 1024
TDEV = 1024
ITERS = 3
MAXT = 12
NS = 32768
NT = 16384
N_SRC = 32
N_TGT = 16


def tile_plan(key):
    src_blocks = SDEV // BLK
    tgt_blocks = TDEV // BLK
    pair_total = src_blocks * tgt_blocks
    covered = max(src_blocks, tgt_blocks)
    device_total = N_SRC * N_TGT
    subkeys = jax.random.split(jax.random.fold_in(key, 7), 5)
    shifts = jax.random.randint(subkeys[0], (device_total, 1), 0, tgt_blocks)
    ranking = jax.vmap(lambda single: jax.random.permutation(single, pair_total))(jax.random.split(subkeys[1], device_total)).astype(jnp.int32)
    cover_index = jnp.arange(covered, dtype=jnp.int32)
    cover_codes = (cover_index % src_blocks)[None, :] * tgt_blocks + (cover_index[None, :] + shifts) % tgt_blocks
    in_cover = jnp.any(cover_codes[:, :, None] == jnp.arange(pair_total, dtype=jnp.int32)[None, None, :], axis=1)
    priority = jnp.where(in_cover, -1, ranking)
    chosen = jnp.argsort(priority, axis=1, stable=True)[:, :MAXT].astype(jnp.int32)
    spare_slots = MAXT - covered
    draw_one = jax.random.randint(subkeys[2], (device_total,), 0, spare_slots + 1)
    draw_two = jax.random.randint(subkeys[3], (device_total,), 0, spare_slots + 1)
    tile_counts = covered + jnp.minimum(draw_one, draw_two)
    busiest = jax.random.randint(subkeys[4], (), 0, device_total)
    tile_counts = jnp.where(jnp.arange(device_total) == busiest, MAXT, tile_counts).astype(jnp.int32)
    tile_slots = jnp.where(jnp.arange(MAXT, dtype=jnp.int32)[None, :] < tile_counts[:, None], chosen, -1)
    return (tile_slots.reshape(N_SRC, N_TGT * MAXT).astype(jnp.int32), tile_counts.reshape(N_SRC, N_TGT))


def draw_tile_list(key, part):
    return tile_plan(key)[0]


def draw_tile_count(key, part):
    return tile_plan(key)[1]


def draw_source_order(key, part):
    key = jax.random.fold_in(key, 3)
    shard_keys = jax.random.split(key, N_SRC)
    shuffled = jax.vmap(lambda single: jax.random.permutation(single, SDEV))(shard_keys)
    return shuffled.reshape(-1).astype(jnp.int32)


def steps_of(own_key, extent, pieces, least, largest):
    factor_of = 1.0
    for position, shards_of in pieces:
        draws = jax.random.uniform(jax.random.fold_in(jax.random.fold_in(own_key, 6), position), (shards_of,), jnp.float32, least / len(pieces), largest / len(pieces))
        factor_of = factor_of * jnp.repeat(jnp.exp(draws), extent[position] // shards_of).reshape((-1,) + (1,) * (len(extent) - 1 - position))
    return factor_of


def normal_values(own_key, dims, deviation, reach, shards=(), kind=jnp.bfloat16):
    level = steps_of(own_key, dims, shards, -0.22, 0.18) if shards else 1.0
    array = jax.random.normal(own_key, dims, jnp.float32) * deviation * level
    return jnp.minimum(jnp.maximum(array, -reach), reach).astype(kind)


def setup_inputs(seed: int = 0) -> dict:
    arg_keys = jax.random.split(jax.random.key(seed), 8)
    return {
        "source_cells": normal_values(arg_keys[0], (NS, EMB), 1.0, 6.0, ((0, 32),)),
        "target_cells": normal_values(arg_keys[1], (NT, EMB), 1.0, 6.0, ((0, 16),)),
        "source_mass": jnp.clip(jnp.exp(math.log(4.0) - 2.7725887 * jax.random.uniform(arg_keys[2], (NS,), jnp.float32) ** steps_of(arg_keys[2], (NS,), ((0, 32),), -0.2, 0.2)), 0.25, 4.0),
        "target_mass": jnp.clip(jnp.exp(math.log(4.0) - 2.7725887 * jax.random.uniform(arg_keys[3], (NT,), jnp.float32) ** steps_of(arg_keys[3], (NT,), ((0, 16),), -0.2, 0.2)), 0.25, 4.0),
        "source_order": draw_source_order(jax.random.fold_in(arg_keys[7], 71), 0),
        "tile_list": draw_tile_list(jax.random.fold_in(arg_keys[7], 71), 0),
        "tile_count": draw_tile_count(jax.random.fold_in(arg_keys[7], 71), 0),
    }


INVERSE_TEMP = 64.0
MASS_POWER = 0.8
NORM_EPSILON = 1e-06

def normalized(embedded):
    widened = embedded.astype(jnp.float32)
    scaled = widened * lax.rsqrt(lax.optimization_barrier(jnp.mean(widened * widened, axis=1, keepdims=True)) + NORM_EPSILON)
    return scaled.astype(jnp.bfloat16)

def reference(source_cells, target_cells, source_mass, target_mass, source_order, tile_list, tile_count):
    src_blocks = SDEV // BLK
    tgt_blocks = TDEV // BLK
    pair_total = src_blocks * tgt_blocks
    global_rows = (source_order.reshape(N_SRC, SDEV) + (jnp.arange(N_SRC, dtype=jnp.int32) * SDEV)[:, None]).reshape(-1).astype(jnp.int32)
    src_hat = normalized(source_cells[global_rows])
    sorted_mass = source_mass[global_rows].reshape(N_SRC, SDEV)
    tgt_hat = normalized(target_cells)
    tile_codes = tile_list.reshape(N_SRC, N_TGT, MAXT)
    alive = jnp.arange(MAXT, dtype=jnp.int32)[None, None, :] < tile_count[:, :, None]
    matched = (tile_codes[..., None] == jnp.arange(pair_total, dtype=jnp.int32)) & alive[..., None]
    block_mask = jnp.any(matched, axis=2).astype(jnp.float32)
    sharpness = INVERSE_TEMP / EMB

    def kernel_rows(shard):
        src_rows = lax.dynamic_slice_in_dim(src_hat, (shard * SDEV).astype(jnp.int32), SDEV, 0)
        similarity = jnp.dot(src_rows, tgt_hat.T, preferred_element_type=jnp.float32)
        linked = block_mask[shard].reshape(N_TGT, src_blocks, tgt_blocks).transpose(1, 0, 2)
        spread = jnp.broadcast_to(linked[:, None, :, :, None], (src_blocks, BLK, N_TGT, tgt_blocks, BLK)).reshape(SDEV, NT)
        return jnp.exp(similarity * sharpness) * spread
    shard_ids = jnp.arange(N_SRC, dtype=jnp.int32)
    tgt_scale = jnp.ones((NT,), jnp.float32)
    src_scale = jnp.ones((N_SRC, SDEV), jnp.float32)
    for rounds in range(ITERS):
        row_total = lax.map(lambda shard: jnp.dot(kernel_rows(shard), tgt_scale, precision=lax.Precision.HIGHEST), shard_ids)
        src_scale = (sorted_mass / row_total) ** MASS_POWER

        def add_shard(shard, running):
            weights = lax.dynamic_index_in_dim(src_scale, shard, 0, keepdims=False)
            return running + jnp.dot(weights, kernel_rows(shard), precision=lax.Precision.HIGHEST)
        col_total = lax.fori_loop(0, N_SRC, add_shard, jnp.zeros((NT,), jnp.float32))
        tgt_scale = (target_mass / col_total) ** MASS_POWER

    def project(shard):
        weighted_full = kernel_rows(shard) * tgt_scale[None, :]
        row_mass = lax.optimization_barrier(jnp.sum(weighted_full, axis=1))
        numerator = jnp.dot(weighted_full.astype(jnp.bfloat16), target_cells, preferred_element_type=jnp.float32)
        return (numerator, row_mass)
    numerator, row_mass = lax.map(project, shard_ids)
    numerator = numerator.reshape(NS, EMB)
    row_mass = row_mass.reshape(NS)
    projected_sorted = (numerator / row_mass[:, None]).astype(jnp.bfloat16)
    log_sorted = jnp.log(src_scale.reshape(NS)) + jnp.log(row_mass)
    projected = jnp.zeros((NS, EMB), jnp.bfloat16).at[global_rows].set(projected_sorted)
    log_mass = jnp.zeros((NS,), jnp.float32).at[global_rows].set(log_sorted)
    return (projected, log_mass)
```

```python
import functools

import jax
import jax.numpy as jnp
from jax import lax
from jax.experimental import pallas as pl
from jax.experimental.pallas import tpu as pltpu
from jax.sharding import PartitionSpec as P

EMB = 512
BLK = 256
ROWS = 1024
COLS = 1024
ITERS = 3
INVERSE_TEMP = 64.0
MASS_POWER = 0.8
NORM_EPSILON = 1e-06
SHARPNESS = INVERSE_TEMP / EMB
SLOTS = 12
OUT = 64
MESH = pl.DeviceIdType.MESH


def normalize_into(cells, hat):
    def step(i, carry):
        rows = pl.ds(i * BLK, BLK)
        wide = cells[rows, :].astype(jnp.float32)
        mean = jnp.sum(wide * wide, axis=1, keepdims=True) * (1.0 / EMB)
        hat[rows, :] = (wide * lax.rsqrt(mean + NORM_EPSILON)).astype(jnp.bfloat16)
        return carry

    lax.fori_loop(0, ROWS // BLK, step, 0)


def power(x):
    return jnp.exp(MASS_POWER * jnp.log(x))


def as_row(tile):
    return jnp.concatenate([tile[k : k + 1, :] for k in range(8)], axis=1)


def split_rows(tile):
    which = lax.broadcasted_iota(jnp.int32, (8, 128), 0)
    pieces = []
    for k in range(8):
        value = jnp.broadcast_to(tile[k : k + 1, :], (8, 128))
        high = value.astype(jnp.bfloat16).astype(jnp.float32)
        piece = jnp.where(which == 0, high, jnp.where(which == 1, value - high, 0.0))
        pieces.append(piece.astype(jnp.bfloat16))
    return jnp.concatenate(pieces, axis=1)


def as_tile(rows):
    which = lax.broadcasted_iota(jnp.int32, (8, 128), 0)
    tile = jnp.zeros((8, 128), jnp.float32)
    for k in range(8):
        piece = jnp.sum(rows[:, k * 128 : (k + 1) * 128], axis=0, keepdims=True)
        tile = jnp.where(which == k, piece, tile)
    return tile


def kernel(
    n_z,
    src_ref,
    tgt_ref,
    smass_ref,
    tmass_ref,
    order_ref,
    list_ref,
    count_ref,
    proj_ref,
    log_ref,
    src_hat,
    tgt_hat,
    k_wide,
    k_half,
    scaled,
    outbox,
    plane_in,
    z_in,
    core_in,
    num,
    relay_p,
    relay_m,
    from_m,
    from_p,
    relay2_p,
    relay2_m,
    from2_m,
    from2_p,
    small_send,
    small_recv,
    big_send,
    big_recv,
):
    s = lax.axis_index("src")
    t = lax.axis_index("tgt")
    z = s // 2
    core = s % 2
    y = t // 4
    x = t % 4

    plane_steps = [(dy, dx) for dy in range(4) for dx in range(4) if (dy, dx) != (0, 0)]
    plane_steps.sort(key=lambda d: -(min(d[0], 4 - d[0]) + min(d[1], 4 - d[1])))
    plane_peers = [(s, ((y + dy) % 4) * 4 + (x + dx) % 4) for dy, dx in plane_steps]
    z_steps = sorted(range(1, n_z), key=lambda d: -min(d, n_z - d))
    z_peers = [(((z + d) % n_z) * 2 + core, t) for d in z_steps]
    sibling = (z * 2 + 1 - core, t)

    def device(where):
        return {"src": where[0], "tgt": where[1]}

    barrier = pltpu.get_barrier_semaphore()
    everyone = z_peers + plane_peers + [sibling]
    for where in everyone:
        pl.semaphore_signal(barrier, 1, device_id=device(where), device_id_type=MESH)

    bits = jnp.int32(0)
    total = count_ref[0, 0]
    for slot in range(SLOTS):
        code = jnp.maximum(list_ref[0, slot], 0)
        bits = bits | jnp.where(slot < total, jnp.int32(1) << code, 0)
    position = lax.broadcasted_iota(jnp.int32, (1, ROWS), 1)
    bits_row = jnp.full((1, ROWS), bits, jnp.int32)
    nibble = (lax.shift_right_logical(bits_row, (position // BLK) * 4) & 15).astype(jnp.float32)

    normalize_into(src_ref, src_hat)
    normalize_into(tgt_ref, tgt_hat)

    def build(i, carry):
        rows = pl.ds(i * BLK, BLK)
        row_ids = lax.broadcasted_iota(jnp.int32, (BLK, 1), 0) + i * BLK
        placed = jnp.where(order_ref[...] == row_ids, nibble, 0.0)
        links = jnp.sum(placed, axis=1, keepdims=True).astype(jnp.int32)
        for q in range(COLS // BLK):
            cols = pl.ds(q * BLK, BLK)
            similarity = lax.dot_general(
                src_hat[rows, :],
                tgt_hat[cols, :],
                (((1,), (1,)), ((), ())),
                preferred_element_type=jnp.float32,
            )
            linked = (lax.shift_right_logical(links, q) & 1).astype(jnp.float32)
            tile = jnp.exp(similarity * SHARPNESS) * linked
            k_wide[rows, cols] = tile
            k_half[rows, cols] = tile.astype(jnp.bfloat16)
        return carry

    lax.fori_loop(0, ROWS // BLK, build, 0)

    def row_product(tile):
        return as_tile(
            lax.dot_general(
                split_rows(tile),
                k_half[...],
                (((1,), (1,)), ((), ())),
                preferred_element_type=jnp.float32,
            )
        )

    def col_product(tile):
        return as_tile(
            jnp.dot(split_rows(tile), k_half[...], preferred_element_type=jnp.float32)
        )

    def broadcast(box, inbox, peers, sem):
        for slot, where in enumerate(peers):
            pltpu.make_async_remote_copy(
                src_ref=outbox.at[box],
                dst_ref=inbox.at[slot],
                send_sem=small_send.at[sem],
                recv_sem=small_recv.at[sem],
                device_id=device(where),
                device_id_type=MESH,
            ).start()

    def arrived(inbox, sem):
        pltpu.make_async_copy(inbox, inbox, small_recv.at[sem]).wait()

    def sent(inbox, sem):
        pltpu.make_async_copy(inbox, inbox, small_send.at[sem]).wait()

    tgt_scale = jnp.ones((8, 128), jnp.float32)
    src_scale = jnp.ones((8, 128), jnp.float32)
    pl.semaphore_wait(barrier, len(everyone))
    for i in range(ITERS):
        mine = row_product(tgt_scale)
        outbox[3 * i] = mine
        broadcast(3 * i, plane_in.at[i], plane_peers, 3 * i)
        arrived(plane_in.at[i], 3 * i)
        src_scale = power(smass_ref[...] / (mine + jnp.sum(plane_in[i], axis=0)))

        mine = col_product(src_scale)
        outbox[3 * i + 1] = mine
        broadcast(3 * i + 1, z_in.at[i], z_peers, 3 * i + 1)
        arrived(z_in.at[i], 3 * i + 1)
        mine = mine + jnp.sum(z_in[i], axis=0)
        outbox[3 * i + 2] = mine
        broadcast(3 * i + 2, core_in.at[i], [sibling], 3 * i + 2)
        arrived(core_in.at[i], 3 * i + 2)
        tgt_scale = power(tmass_ref[...] / (mine + core_in[i, 0]))

    a = jnp.where(core == 0, x, y)
    b = jnp.where(core == 0, y, x)
    step_a = 1 + 3 * core
    step_b = 4 - 3 * core

    def at(a_now, b_now):
        return (s, (a_now % 4) * step_a + (b_now % 4) * step_b)

    tgt_row = as_row(tgt_scale)

    def numerators(d):
        for e in range(4):
            chunk = ((a + d) % 4) * step_a + e * step_b
            weighted = k_wide[pl.ds(chunk * OUT, OUT), :] * tgt_row
            scaled[e * OUT : (e + 1) * OUT, :] = weighted.astype(jnp.bfloat16)
        num[d] = jnp.dot(
            scaled[...], tgt_ref[...], preferred_element_type=jnp.float32
        ).reshape(4, OUT, EMB)

    def send(src, dst, where, sem):
        copy = pltpu.make_async_remote_copy(
            src_ref=src,
            dst_ref=dst,
            send_sem=big_send.at[sem],
            recv_sem=big_recv.at[sem],
            device_id=device(where),
            device_id_type=MESH,
        )
        copy.start()
        return copy

    a_next, a_last = at(a + 1, b), at(a - 1, b)
    b_next, b_last = at(a, b + 1), at(a, b - 1)
    numerators(2)
    first_p = send(num.at[2, 0:2], relay_p, a_next, 0)
    first_m = send(num.at[2, 2:4], relay_m, a_last, 1)
    numerators(1)
    direct_p = send(num.at[1, 2:4], from_m.at[2:4], a_next, 2)
    numerators(3)
    direct_m = send(num.at[3, 0:2], from_p.at[0:2], a_last, 3)

    mass = row_product(tgt_scale)
    outbox[9] = mass
    broadcast(9, plane_in.at[3], plane_peers, 9)

    first_p.wait_recv()
    num[1, 0:2] = num[1, 0:2] + relay_p[...]
    second_p = send(num.at[1, 0:2], from_m.at[0:2], a_next, 4)
    first_m.wait_recv()
    num[3, 2:4] = num[3, 2:4] + relay_m[...]
    second_m = send(num.at[3, 2:4], from_p.at[2:4], a_last, 5)
    numerators(0)
    direct_p.wait_recv()
    direct_m.wait_recv()
    second_p.wait_recv()
    second_m.wait_recv()
    num[0] = num[0] + from_m[...] + from_p[...]

    half = OUT // 2
    up, down, over = (b + 1) % 4, (b + 3) % 4, (b + 2) % 4
    far_p = send(num.at[0, over, 0:half], relay2_p, b_next, 6)
    far_m = send(num.at[0, over, half:OUT], relay2_m, b_last, 7)
    near_p = send(num.at[0, up, half:OUT], from2_m.at[half:OUT], b_next, 8)
    near_m = send(num.at[0, down, 0:half], from2_p.at[0:half], b_last, 9)
    far_p.wait_recv()
    num[0, up, 0:half] = num[0, up, 0:half] + relay2_p[...]
    last_p = send(num.at[0, up, 0:half], from2_m.at[0:half], b_next, 10)
    far_m.wait_recv()
    num[0, down, half:OUT] = num[0, down, half:OUT] + relay2_m[...]
    last_m = send(num.at[0, down, half:OUT], from2_p.at[half:OUT], b_last, 11)

    arrived(plane_in.at[3], 9)
    mass = mass + jnp.sum(plane_in[3], axis=0)
    logs = jnp.log(src_scale) + jnp.log(mass)
    sub = lax.broadcasted_iota(jnp.int32, (8, 128), 0)
    mine_now = sub == t // 2
    log_row = jnp.sum(jnp.where(mine_now, logs, 0.0), axis=0, keepdims=True)
    mass_row = jnp.sum(jnp.where(mine_now, mass, 0.0), axis=0, keepdims=True)
    odd = jnp.full((1, OUT), t % 2, jnp.int32) == 1
    log_ref[...] = jnp.where(odd, log_row[:, OUT:], log_row[:, :OUT])
    row_id = lax.broadcasted_iota(jnp.int32, (OUT, 128), 0) + (t % 2) * OUT
    lane_id = lax.broadcasted_iota(jnp.int32, (OUT, 128), 1)
    mass_col = jnp.sum(jnp.where(row_id == lane_id, mass_row, 0.0), axis=1, keepdims=True)

    near_p.wait_recv()
    near_m.wait_recv()
    last_p.wait_recv()
    last_m.wait_recv()
    final = num[0, b] + from2_m[...] + from2_p[...]
    proj_ref[...] = (final / mass_col).astype(jnp.bfloat16)

    for i in range(ITERS):
        sent(plane_in.at[i], 3 * i)
        sent(z_in.at[i], 3 * i + 1)
        sent(core_in.at[i], 3 * i + 2)
    sent(plane_in.at[3], 9)
    for copy in (first_p, first_m, direct_p, direct_m, second_p, second_m):
        copy.wait_send()
    for copy in (far_p, far_m, near_p, near_m, last_p, last_m):
        copy.wait_send()


def body(n_z, source_cells, target_cells, source_mass, target_mass, source_order, tile_list, tile_count):
    vmem = pl.BlockSpec(memory_space=pltpu.VMEM)
    smem = pl.BlockSpec(memory_space=pltpu.SMEM)
    half = OUT // 2
    f32, bf16 = jnp.float32, jnp.bfloat16
    projected, log_mass = pl.pallas_call(
        functools.partial(kernel, n_z),
        out_shape=(
            jax.ShapeDtypeStruct((OUT, EMB), bf16),
            jax.ShapeDtypeStruct((1, OUT), f32),
        ),
        in_specs=[vmem] * 5 + [smem] * 2,
        out_specs=(vmem, vmem),
        scratch_shapes=[
            pltpu.VMEM((ROWS, EMB), bf16),
            pltpu.VMEM((COLS, EMB), bf16),
            pltpu.VMEM((ROWS, COLS), f32),
            pltpu.VMEM((ROWS, COLS), bf16),
            pltpu.VMEM((BLK, COLS), bf16),
            pltpu.VMEM((10, 8, 128), f32),
            pltpu.VMEM((4, 15, 8, 128), f32),
            pltpu.VMEM((3, n_z - 1, 8, 128), f32),
            pltpu.VMEM((3, 1, 8, 128), f32),
            pltpu.VMEM((4, 4, OUT, EMB), f32),
            pltpu.VMEM((2, OUT, EMB), f32),
            pltpu.VMEM((2, OUT, EMB), f32),
            pltpu.VMEM((4, OUT, EMB), f32),
            pltpu.VMEM((4, OUT, EMB), f32),
            pltpu.VMEM((half, EMB), f32),
            pltpu.VMEM((half, EMB), f32),
            pltpu.VMEM((OUT, EMB), f32),
            pltpu.VMEM((OUT, EMB), f32),
            pltpu.SemaphoreType.DMA((10,)),
            pltpu.SemaphoreType.DMA((10,)),
            pltpu.SemaphoreType.DMA((12,)),
            pltpu.SemaphoreType.DMA((12,)),
        ],
        compiler_params=pltpu.CompilerParams(
            collective_id=0, has_side_effects=True, vmem_limit_bytes=48 * 1024 * 1024
        ),
    )(
        source_cells,
        target_cells,
        source_mass.reshape(8, 128),
        target_mass.reshape(8, 128),
        source_order.reshape(1, ROWS),
        tile_list,
        tile_count,
    )
    return projected, log_mass.reshape(OUT)


def solution(mesh):
    placed = (
        P("src", None),
        P("tgt", None),
        P("src"),
        P("tgt"),
        P("src"),
        P("src", "tgt"),
        P("src", "tgt"),
    )
    return jax.shard_map(
        functools.partial(body, mesh.shape["src"] // 2),
        mesh=mesh,
        in_specs=placed,
        out_specs=(P(("src", "tgt"), None), P(("src", "tgt"))),
        check_vma=False,
    )
```

```python
import functools

import jax
import jax.numpy as jnp
from jax import lax
from jax.experimental import pallas as pl
from jax.experimental.pallas import tpu as pltpu
from jax.sharding import PartitionSpec as P

EMB = 512
BLK = 256
ROWS = 1024
COLS = 1024
ITERS = 3
INVERSE_TEMP = 64.0
MASS_POWER = 0.8
NORM_EPSILON = 1e-06
SHARPNESS = INVERSE_TEMP / EMB
SLOTS = 12
OUT = 64
WIDE = EMB // 2
FAR = 8
MESH = pl.DeviceIdType.MESH


def normalize_into(cells, hat):
    def step(i, carry):
        rows = pl.ds(i * BLK, BLK)
        wide = cells[rows, :].astype(jnp.float32)
        mean = jnp.sum(wide * wide, axis=1, keepdims=True) * (1.0 / EMB)
        hat[rows, :] = (wide * lax.rsqrt(mean + NORM_EPSILON)).astype(jnp.bfloat16)
        return carry

    lax.fori_loop(0, ROWS // BLK, step, 0)


def power(x):
    return jnp.exp(MASS_POWER * jnp.log(x))


def as_row(tile):
    return jnp.concatenate([tile[k : k + 1, :] for k in range(8)], axis=1)


def split_rows(tile):
    which = lax.broadcasted_iota(jnp.int32, (8, 128), 0)
    pieces = []
    for k in range(8):
        value = jnp.broadcast_to(tile[k : k + 1, :], (8, 128))
        high = value.astype(jnp.bfloat16).astype(jnp.float32)
        piece = jnp.where(which == 0, high, jnp.where(which == 1, value - high, 0.0))
        pieces.append(piece.astype(jnp.bfloat16))
    return jnp.concatenate(pieces, axis=1)


def as_tile(rows):
    which = lax.broadcasted_iota(jnp.int32, (8, 128), 0)
    tile = jnp.zeros((8, 128), jnp.float32)
    for k in range(8):
        piece = jnp.sum(rows[:, k * 128 : (k + 1) * 128], axis=0, keepdims=True)
        tile = jnp.where(which == k, piece, tile)
    return tile


def kernel(
    n_z,
    src_hbm,
    tgt_hbm,
    smass_hbm,
    tmass_hbm,
    order_hbm,
    list_hbm,
    proj_ref,
    log_ref,
    src_ref,
    tgt_ref,
    smass_ref,
    tmass_ref,
    order_ref,
    list_ref,
    src_hat,
    tgt_hat,
    k_wide,
    k_half,
    k_turned,
    scaled,
    outbox,
    plane_in,
    far_in,
    near_in,
    core_in,
    num,
    relay_p,
    relay_m,
    from_m,
    from_p,
    relay2_p,
    relay2_m,
    from2_m,
    from2_p,
    over2,
    load_sem,
    small_send,
    small_recv,
    big_send,
    big_recv,
):
    s = lax.axis_index("src")
    t = lax.axis_index("tgt")
    z = s // 2
    core = s % 2
    y = t // 4
    x = t % 4

    plane_steps = [(dy, dx) for dy in range(4) for dx in range(4) if (dy, dx) != (0, 0)]
    plane_steps.sort(key=lambda d: -(min(d[0], 4 - d[0]) + min(d[1], 4 - d[1])))
    plane_peers = [(s, ((y + dy) % 4) * 4 + (x + dx) % 4) for dy, dx in plane_steps]
    z_steps = sorted(range(1, n_z), key=lambda d: -min(d, n_z - d))
    far_steps = [d for d in z_steps if min(d, n_z - d) >= FAR]
    near_steps = [d for d in z_steps if min(d, n_z - d) < FAR]
    far_peers = [
        (((z + d) % n_z) * 2 + side, t) for d in far_steps for side in (core, 1 - core)
    ]
    near_peers = [(((z + d) % n_z) * 2 + core, t) for d in near_steps]
    sibling = (z * 2 + 1 - core, t)

    def device(where):
        return {"src": where[0], "tgt": where[1]}

    barrier = pltpu.get_barrier_semaphore()
    everyone = far_peers + near_peers + plane_peers + [sibling]
    for where in everyone:
        pl.semaphore_signal(barrier, 1, device_id=device(where), device_id_type=MESH)
    loads = [
        pltpu.make_async_copy(there, here, load_sem.at[i])
        for i, (there, here) in enumerate(
            (
                (src_hbm, src_ref),
                (tgt_hbm, tgt_ref),
                (order_hbm, order_ref),
                (list_hbm, list_ref),
                (smass_hbm, smass_ref),
                (tmass_hbm, tmass_ref),
            )
        )
    ]
    for load in loads:
        load.start()
    loads[0].wait()
    normalize_into(src_ref, src_hat)
    loads[1].wait()
    normalize_into(tgt_ref, tgt_hat)
    for load in loads[2:]:
        load.wait()

    codes = jnp.maximum(list_ref[...], 0)
    live = list_ref[...] >= 0
    flags = jnp.where(live, jnp.int32(1) << codes, 0).astype(jnp.float32)
    bits = jnp.sum(flags, axis=1, keepdims=True).astype(jnp.int32)
    position = lax.broadcasted_iota(jnp.int32, (1, ROWS), 1)
    bits_row = jnp.broadcast_to(bits, (1, ROWS))
    nibble = (lax.shift_right_logical(bits_row, (position // BLK) * 4) & 15).astype(jnp.float32)

    def build(i, carry):
        rows = pl.ds(i * BLK, BLK)
        row_ids = lax.broadcasted_iota(jnp.int32, (BLK, 1), 0) + i * BLK
        placed = jnp.where(order_ref[...] == row_ids, nibble, 0.0)
        links = jnp.sum(placed, axis=1, keepdims=True).astype(jnp.int32)
        for q in range(COLS // BLK):
            cols = pl.ds(q * BLK, BLK)
            similarity = lax.dot_general(
                src_hat[rows, :],
                tgt_hat[cols, :],
                (((1,), (1,)), ((), ())),
                preferred_element_type=jnp.float32,
            )
            linked = (lax.shift_right_logical(links, q) & 1).astype(jnp.float32)
            tile = jnp.exp(similarity * SHARPNESS) * linked
            k_wide[rows, cols] = tile
            k_half[rows, cols] = tile.astype(jnp.bfloat16)
        return carry

    lax.fori_loop(0, ROWS // BLK, build, 0)

    def turn(i, carry):
        rows = pl.ds(i * BLK, BLK)
        for q in range(COLS // BLK):
            cols = pl.ds(q * BLK, BLK)
            k_turned[cols, rows] = jnp.transpose(k_wide[rows, cols]).astype(jnp.bfloat16)
        return carry

    def first_row_product(tile):
        return as_tile(
            lax.dot_general(
                split_rows(tile),
                k_half[...],
                (((1,), (1,)), ((), ())),
                preferred_element_type=jnp.float32,
            )
        )

    def row_product(tile):
        return as_tile(
            jnp.dot(split_rows(tile), k_turned[...], preferred_element_type=jnp.float32)
        )

    def col_product(tile):
        return as_tile(
            jnp.dot(split_rows(tile), k_half[...], preferred_element_type=jnp.float32)
        )

    def broadcast(box, inbox, peers, sem):
        for slot, where in enumerate(peers):
            pltpu.make_async_remote_copy(
                src_ref=outbox.at[box],
                dst_ref=inbox.at[slot],
                send_sem=small_send.at[sem],
                recv_sem=small_recv.at[sem],
                device_id=device(where),
                device_id_type=MESH,
            ).start()

    def arrived(inbox, sem):
        pltpu.make_async_copy(inbox, inbox, small_recv.at[sem]).wait()

    def sent(inbox, sem):
        pltpu.make_async_copy(inbox, inbox, small_send.at[sem]).wait()

    tgt_scale = jnp.ones((8, 128), jnp.float32)
    src_scale = jnp.ones((8, 128), jnp.float32)
    pl.semaphore_wait(barrier, len(everyone))
    for i in range(ITERS):
        mine = row_product(tgt_scale) if i else first_row_product(tgt_scale)
        outbox[3 * i] = mine
        broadcast(3 * i, plane_in.at[i], plane_peers, 4 * i)
        if i == 0:
            lax.fori_loop(0, ROWS // BLK, turn, 0)
        arrived(plane_in.at[i], 4 * i)
        src_scale = power(smass_ref[...] / (mine + jnp.sum(plane_in[i], axis=0)))

        mine = col_product(src_scale)
        outbox[3 * i + 1] = mine
        broadcast(3 * i + 1, far_in.at[i], far_peers, 4 * i + 1)
        broadcast(3 * i + 1, near_in.at[i], near_peers, 4 * i + 2)
        arrived(near_in.at[i], 4 * i + 2)
        mine = mine + jnp.sum(near_in[i], axis=0)
        outbox[3 * i + 2] = mine
        broadcast(3 * i + 2, core_in.at[i], [sibling], 4 * i + 3)
        arrived(far_in.at[i], 4 * i + 1)
        mine = mine + jnp.sum(far_in[i], axis=0)
        arrived(core_in.at[i], 4 * i + 3)
        tgt_scale = power(tmass_ref[...] / (mine + core_in[i, 0]))

    a = jnp.where(core == 0, x, y)
    b = jnp.where(core == 0, y, x)
    step_a = 1 + 3 * core
    step_b = 4 - 3 * core

    def at(a_now, b_now):
        return (s, (a_now % 4) * step_a + (b_now % 4) * step_b)

    tgt_row = as_row(tgt_scale)

    def scale_rows(d):
        for e in range(4):
            chunk = ((a + d) % 4) * step_a + e * step_b
            weighted = k_wide[pl.ds(chunk * OUT, OUT), :] * tgt_row
            scaled[e * OUT : (e + 1) * OUT, :] = weighted.astype(jnp.bfloat16)

    def numerators(d, h):
        num[h, d] = jnp.dot(
            scaled[...],
            tgt_ref[:, h * WIDE : (h + 1) * WIDE],
            preferred_element_type=jnp.float32,
        ).reshape(4, OUT, WIDE)

    started = []

    def send(src, dst, where):
        sem = len(started)
        copy = pltpu.make_async_remote_copy(
            src_ref=src,
            dst_ref=dst,
            send_sem=big_send.at[sem],
            recv_sem=big_recv.at[sem],
            device_id=device(where),
            device_id_type=MESH,
        )
        copy.start()
        started.append(copy)
        return copy

    a_next, a_last = at(a + 1, b), at(a - 1, b)
    b_next, b_last, b_over = at(a, b + 1), at(a, b - 1), at(a, b + 2)
    first_p, first_m, direct, second = {}, {}, {}, {}
    scale_rows(2)
    for h in range(2):
        numerators(2, h)
        first_p[h] = send(num.at[h, 2, 0:2], relay_p.at[h], a_next)
        first_m[h] = send(num.at[h, 2, 2:4], relay_m.at[h], a_last)
    scale_rows(1)
    for h in range(2):
        numerators(1, h)
        direct[h] = [send(num.at[h, 1, 2:4], from_m.at[h, 2:4], a_next)]
    scale_rows(3)
    for h in range(2):
        numerators(3, h)
        direct[h].append(send(num.at[h, 3, 0:2], from_p.at[h, 0:2], a_last))

    for h in range(2):
        first_p[h].wait_recv()
        num[h, 1, 0:2] = num[h, 1, 0:2] + relay_p[h]
        second[h] = [send(num.at[h, 1, 0:2], from_m.at[h, 0:2], a_next)]
        first_m[h].wait_recv()
        num[h, 3, 2:4] = num[h, 3, 2:4] + relay_m[h]
        second[h].append(send(num.at[h, 3, 2:4], from_p.at[h, 2:4], a_last))

    mass = row_product(tgt_scale)
    outbox[9] = mass
    broadcast(9, plane_in.at[3], plane_peers, 12)

    scale_rows(0)
    for h in range(2):
        numerators(0, h)

    def gather(h):
        for copy in direct[h] + second[h]:
            copy.wait_recv()
        num[h, 0] = num[h, 0] + from_m[h] + from_p[h]

    half = OUT // 2
    up, down, over = (b + 1) % 4, (b + 3) % 4, (b + 2) % 4
    gather(0)
    far_p = send(num.at[0, 0, over, 0:half], relay2_p, b_next)
    far_m = send(num.at[0, 0, over, half:OUT], relay2_m, b_last)
    ends = [
        send(num.at[0, 0, up, half:OUT], from2_m.at[0, half:OUT], b_next),
        send(num.at[0, 0, down, 0:half], from2_p.at[0, 0:half], b_last),
    ]
    gather(1)
    ends.append(send(num.at[1, 0, over], over2, b_over))
    ends.append(send(num.at[1, 0, up], from2_m.at[1], b_next))
    ends.append(send(num.at[1, 0, down], from2_p.at[1], b_last))
    far_p.wait_recv()
    num[0, 0, up, 0:half] = num[0, 0, up, 0:half] + relay2_p[...]
    ends.append(send(num.at[0, 0, up, 0:half], from2_m.at[0, 0:half], b_next))
    far_m.wait_recv()
    num[0, 0, down, half:OUT] = num[0, 0, down, half:OUT] + relay2_m[...]
    ends.append(send(num.at[0, 0, down, half:OUT], from2_p.at[0, half:OUT], b_last))

    arrived(plane_in.at[3], 12)
    mass = mass + jnp.sum(plane_in[3], axis=0)
    logs = jnp.log(src_scale) + jnp.log(mass)
    sub = lax.broadcasted_iota(jnp.int32, (8, 128), 0)
    mine_now = sub == t // 2
    log_row = jnp.sum(jnp.where(mine_now, logs, 0.0), axis=0, keepdims=True)
    mass_row = jnp.sum(jnp.where(mine_now, mass, 0.0), axis=0, keepdims=True)
    odd = jnp.full((1, OUT), t % 2, jnp.int32) == 1
    log_ref[...] = jnp.where(odd, log_row[:, OUT:], log_row[:, :OUT])
    row_id = lax.broadcasted_iota(jnp.int32, (OUT, 128), 0) + (t % 2) * OUT
    lane_id = lax.broadcasted_iota(jnp.int32, (OUT, 128), 1)
    mass_col = jnp.sum(jnp.where(row_id == lane_id, mass_row, 0.0), axis=1, keepdims=True)

    for copy in ends:
        copy.wait_recv()
    final = num[0, 0, b] + from2_m[0] + from2_p[0]
    proj_ref[:, 0:WIDE] = (final / mass_col).astype(jnp.bfloat16)
    final = num[1, 0, b] + from2_m[1] + from2_p[1] + over2[...]
    proj_ref[:, WIDE:EMB] = (final / mass_col).astype(jnp.bfloat16)

    for i in range(ITERS):
        sent(plane_in.at[i], 4 * i)
        sent(far_in.at[i], 4 * i + 1)
        sent(near_in.at[i], 4 * i + 2)
        sent(core_in.at[i], 4 * i + 3)
    sent(plane_in.at[3], 12)
    for copy in started:
        copy.wait_send()


def body(n_z, source_cells, target_cells, source_mass, target_mass, source_order, tile_list, tile_count):
    vmem = pl.BlockSpec(memory_space=pltpu.VMEM)
    hbm = pl.BlockSpec(memory_space=pltpu.HBM)
    half = OUT // 2
    near = len([d for d in range(1, n_z) if min(d, n_z - d) < FAR])
    far = 2 * (n_z - 1 - near)
    f32, bf16, i32 = jnp.float32, jnp.bfloat16, jnp.int32
    projected, log_mass = pl.pallas_call(
        functools.partial(kernel, n_z),
        out_shape=(
            jax.ShapeDtypeStruct((OUT, EMB), bf16),
            jax.ShapeDtypeStruct((1, OUT), f32),
        ),
        in_specs=[hbm] * 6,
        out_specs=(vmem, vmem),
        scratch_shapes=[
            pltpu.VMEM((ROWS, EMB), bf16),
            pltpu.VMEM((COLS, EMB), bf16),
            pltpu.VMEM((8, 128), f32),
            pltpu.VMEM((8, 128), f32),
            pltpu.VMEM((1, ROWS), i32),
            pltpu.VMEM((1, SLOTS), i32),
            pltpu.VMEM((ROWS, EMB), bf16),
            pltpu.VMEM((COLS, EMB), bf16),
            pltpu.VMEM((ROWS, COLS), f32),
            pltpu.VMEM((ROWS, COLS), bf16),
            pltpu.VMEM((COLS, ROWS), bf16),
            pltpu.VMEM((BLK, COLS), bf16),
            pltpu.VMEM((10, 8, 128), f32),
            pltpu.VMEM((4, 15, 8, 128), f32),
            pltpu.VMEM((3, far, 8, 128), f32),
            pltpu.VMEM((3, near, 8, 128), f32),
            pltpu.VMEM((3, 1, 8, 128), f32),
            pltpu.VMEM((2, 4, 4, OUT, WIDE), f32),
            pltpu.VMEM((2, 2, OUT, WIDE), f32),
            pltpu.VMEM((2, 2, OUT, WIDE), f32),
            pltpu.VMEM((2, 4, OUT, WIDE), f32),
            pltpu.VMEM((2, 4, OUT, WIDE), f32),
            pltpu.VMEM((half, WIDE), f32),
            pltpu.VMEM((half, WIDE), f32),
            pltpu.VMEM((2, OUT, WIDE), f32),
            pltpu.VMEM((2, OUT, WIDE), f32),
            pltpu.VMEM((OUT, WIDE), f32),
            pltpu.SemaphoreType.DMA((6,)),
            pltpu.SemaphoreType.DMA((13,)),
            pltpu.SemaphoreType.DMA((13,)),
            pltpu.SemaphoreType.DMA((21,)),
            pltpu.SemaphoreType.DMA((21,)),
        ],
        compiler_params=pltpu.CompilerParams(
            collective_id=0, has_side_effects=True, vmem_limit_bytes=64 * 1024 * 1024
        ),
    )(
        source_cells,
        target_cells,
        source_mass.reshape(8, 128),
        target_mass.reshape(8, 128),
        source_order.reshape(1, ROWS),
        tile_list,
    )
    return projected, log_mass.reshape(OUT)


def solution(mesh):
    placed = (
        P("src", None),
        P("tgt", None),
        P("src"),
        P("tgt"),
        P("src"),
        P("src", "tgt"),
        P("src", "tgt"),
    )
    return jax.shard_map(
        functools.partial(body, mesh.shape["src"] // 2),
        mesh=mesh,
        in_specs=placed,
        out_specs=(P(("src", "tgt"), None), P(("src", "tgt"))),
        check_vma=False,
    )
```

```python
import functools

import jax
import jax.numpy as jnp
from jax import lax
from jax.experimental import pallas as pl
from jax.experimental.pallas import tpu as pltpu
from jax.sharding import PartitionSpec as P

EMB = 512
BLK = 256
ROWS = 1024
COLS = 1024
ITERS = 3
INVERSE_TEMP = 64.0
MASS_POWER = 0.8
NORM_EPSILON = 1e-06
SHARPNESS = INVERSE_TEMP / EMB
SLOTS = 12
OUT = 64
WIDE = EMB // 2
FAR = 8
MESH = pl.DeviceIdType.MESH


def normalize_into(cells, hat):
    def step(i, carry):
        rows = pl.ds(i * BLK, BLK)
        wide = cells[rows, :].astype(jnp.float32)
        mean = jnp.sum(wide * wide, axis=1, keepdims=True) * (1.0 / EMB)
        hat[rows, :] = (wide * lax.rsqrt(mean + NORM_EPSILON)).astype(jnp.bfloat16)
        return carry

    lax.fori_loop(0, ROWS // BLK, step, 0)


def power(x):
    return jnp.exp(MASS_POWER * jnp.log(x))


def as_row(tile):
    return jnp.concatenate([tile[k : k + 1, :] for k in range(8)], axis=1)


def split_rows(tile):
    which = lax.broadcasted_iota(jnp.int32, (8, 128), 0)
    pieces = []
    for k in range(8):
        value = jnp.broadcast_to(tile[k : k + 1, :], (8, 128))
        high = value.astype(jnp.bfloat16).astype(jnp.float32)
        piece = jnp.where(which == 0, high, jnp.where(which == 1, value - high, 0.0))
        pieces.append(piece.astype(jnp.bfloat16))
    return jnp.concatenate(pieces, axis=1)


def as_tile(rows):
    which = lax.broadcasted_iota(jnp.int32, (8, 128), 0)
    tile = jnp.zeros((8, 128), jnp.float32)
    for k in range(8):
        piece = jnp.sum(rows[:, k * 128 : (k + 1) * 128], axis=0, keepdims=True)
        tile = jnp.where(which == k, piece, tile)
    return tile


def kernel(
    n_z,
    src_hbm,
    tgt_hbm,
    smass_hbm,
    tmass_hbm,
    order_hbm,
    list_hbm,
    proj_ref,
    log_ref,
    src_ref,
    tgt_ref,
    smass_ref,
    tmass_ref,
    order_ref,
    list_ref,
    src_hat,
    tgt_hat,
    k_wide,
    k_half,
    k_turned,
    scaled,
    outbox,
    plane_in,
    far_in,
    near_in,
    core_in,
    num,
    relay_p,
    relay_m,
    from_m,
    from_p,
    relay2_p,
    relay2_m,
    from2_m,
    from2_p,
    over2,
    load_sem,
    small_send,
    small_recv,
    big_send,
    big_recv,
):
    s = lax.axis_index("src")
    t = lax.axis_index("tgt")
    z = s // 2
    core = s % 2
    y = t // 4
    x = t % 4

    plane_steps = [(dy, dx) for dy in range(4) for dx in range(4) if (dy, dx) != (0, 0)]
    plane_steps.sort(key=lambda d: -(min(d[0], 4 - d[0]) + min(d[1], 4 - d[1])))
    plane_peers = [(s, ((y + dy) % 4) * 4 + (x + dx) % 4) for dy, dx in plane_steps]
    z_steps = sorted(range(1, n_z), key=lambda d: -min(d, n_z - d))
    far_steps = [d for d in z_steps if min(d, n_z - d) >= FAR]
    near_steps = [d for d in z_steps if min(d, n_z - d) < FAR]
    far_peers = [
        (((z + d) % n_z) * 2 + side, t) for d in far_steps for side in (core, 1 - core)
    ]
    near_peers = [(((z + d) % n_z) * 2 + core, t) for d in near_steps]
    sibling = (z * 2 + 1 - core, t)

    def device(where):
        return {"src": where[0], "tgt": where[1]}

    barrier = pltpu.get_barrier_semaphore()
    everyone = far_peers + near_peers + plane_peers + [sibling]
    for where in everyone:
        pl.semaphore_signal(barrier, 1, device_id=device(where), device_id_type=MESH)
    loads = [
        pltpu.make_async_copy(there, here, load_sem.at[i])
        for i, (there, here) in enumerate(
            (
                (src_hbm, src_ref),
                (tgt_hbm, tgt_ref),
                (order_hbm, order_ref),
                (list_hbm, list_ref),
                (smass_hbm, smass_ref),
                (tmass_hbm, tmass_ref),
            )
        )
    ]
    for load in loads:
        load.start()
    loads[0].wait()
    normalize_into(src_ref, src_hat)
    loads[1].wait()
    normalize_into(tgt_ref, tgt_hat)
    for load in loads[2:]:
        load.wait()

    codes = jnp.maximum(list_ref[...], 0)
    live = list_ref[...] >= 0
    flags = jnp.where(live, jnp.int32(1) << codes, 0).astype(jnp.float32)
    bits = jnp.sum(flags, axis=1, keepdims=True).astype(jnp.int32)
    position = lax.broadcasted_iota(jnp.int32, (1, ROWS), 1)
    bits_row = jnp.broadcast_to(bits, (1, ROWS))
    nibble = (lax.shift_right_logical(bits_row, (position // BLK) * 4) & 15).astype(jnp.float32)

    def build(i, carry):
        rows = pl.ds(i * BLK, BLK)
        row_ids = lax.broadcasted_iota(jnp.int32, (BLK, 1), 0) + i * BLK
        placed = jnp.where(order_ref[...] == row_ids, nibble, 0.0)
        links = jnp.sum(placed, axis=1, keepdims=True).astype(jnp.int32)
        for q in range(COLS // BLK):
            cols = pl.ds(q * BLK, BLK)
            similarity = lax.dot_general(
                src_hat[rows, :],
                tgt_hat[cols, :],
                (((1,), (1,)), ((), ())),
                preferred_element_type=jnp.float32,
            )
            linked = (lax.shift_right_logical(links, q) & 1).astype(jnp.float32)
            tile = jnp.exp(similarity * SHARPNESS) * linked
            k_wide[rows, cols] = tile
            k_half[rows, cols] = tile.astype(jnp.bfloat16)
        return carry

    lax.fori_loop(0, ROWS // BLK, build, 0)

    def turn(i, carry):
        rows = pl.ds(i * BLK, BLK)
        for q in range(COLS // BLK):
            cols = pl.ds(q * BLK, BLK)
            k_turned[cols, rows] = jnp.transpose(k_wide[rows, cols]).astype(jnp.bfloat16)
        return carry

    def first_row_product(tile):
        return as_tile(
            lax.dot_general(
                split_rows(tile),
                k_half[...],
                (((1,), (1,)), ((), ())),
                preferred_element_type=jnp.float32,
            )
        )

    def row_product(tile):
        return as_tile(
            jnp.dot(split_rows(tile), k_turned[...], preferred_element_type=jnp.float32)
        )

    def col_product(tile):
        return as_tile(
            jnp.dot(split_rows(tile), k_half[...], preferred_element_type=jnp.float32)
        )

    def broadcast(box, inbox, peers, sem):
        for slot, where in enumerate(peers):
            pltpu.make_async_remote_copy(
                src_ref=outbox.at[box],
                dst_ref=inbox.at[slot],
                send_sem=small_send.at[sem],
                recv_sem=small_recv.at[sem],
                device_id=device(where),
                device_id_type=MESH,
            ).start()

    def arrived(inbox, sem):
        pltpu.make_async_copy(inbox, inbox, small_recv.at[sem]).wait()

    def sent(inbox, sem):
        pltpu.make_async_copy(inbox, inbox, small_send.at[sem]).wait()

    tgt_scale = jnp.ones((8, 128), jnp.float32)
    src_scale = jnp.ones((8, 128), jnp.float32)
    pl.semaphore_wait(barrier, len(everyone))
    for i in range(ITERS):
        mine = row_product(tgt_scale) if i else first_row_product(tgt_scale)
        outbox[3 * i] = mine
        broadcast(3 * i, plane_in.at[i], plane_peers, 4 * i)
        if i == 0:
            lax.fori_loop(0, ROWS // BLK, turn, 0)
        arrived(plane_in.at[i], 4 * i)
        src_scale = power(smass_ref[...] / (mine + jnp.sum(plane_in[i], axis=0)))

        mine = col_product(src_scale)
        outbox[3 * i + 1] = mine
        broadcast(3 * i + 1, far_in.at[i], far_peers, 4 * i + 1)
        broadcast(3 * i + 1, near_in.at[i], near_peers, 4 * i + 2)
        arrived(near_in.at[i], 4 * i + 2)
        mine = mine + jnp.sum(near_in[i], axis=0)
        outbox[3 * i + 2] = mine
        broadcast(3 * i + 2, core_in.at[i], [sibling], 4 * i + 3)
        arrived(far_in.at[i], 4 * i + 1)
        mine = mine + jnp.sum(far_in[i], axis=0)
        arrived(core_in.at[i], 4 * i + 3)
        tgt_scale = power(tmass_ref[...] / (mine + core_in[i, 0]))

    a = jnp.where(core == 0, x, y)
    b = jnp.where(core == 0, y, x)
    step_a = 1 + 3 * core
    step_b = 4 - 3 * core

    def at(a_now, b_now):
        return (s, (a_now % 4) * step_a + (b_now % 4) * step_b)

    tgt_row = as_row(tgt_scale)

    def scale_rows(d):
        for e in range(4):
            chunk = ((a + d) % 4) * step_a + e * step_b
            weighted = k_wide[pl.ds(chunk * OUT, OUT), :] * tgt_row
            scaled[e * OUT : (e + 1) * OUT, :] = weighted.astype(jnp.bfloat16)

    def numerators(d, h):
        num[h, d] = jnp.dot(
            scaled[...],
            tgt_ref[:, h * WIDE : (h + 1) * WIDE],
            preferred_element_type=jnp.float32,
        ).reshape(4, OUT, WIDE)

    started = []

    def send(src, dst, where):
        sem = len(started)
        copy = pltpu.make_async_remote_copy(
            src_ref=src,
            dst_ref=dst,
            send_sem=big_send.at[sem],
            recv_sem=big_recv.at[sem],
            device_id=device(where),
            device_id_type=MESH,
        )
        copy.start()
        started.append(copy)
        return copy

    a_next, a_last = at(a + 1, b), at(a - 1, b)
    b_next, b_last, b_over = at(a, b + 1), at(a, b - 1), at(a, b + 2)
    first_p, first_m, direct, second = {}, {}, {}, {}
    scale_rows(2)
    for h in range(2):
        numerators(2, h)
        first_p[h] = send(num.at[h, 2, 0:2], relay_p.at[h], a_next)
        first_m[h] = send(num.at[h, 2, 2:4], relay_m.at[h], a_last)
    scale_rows(1)
    for h in range(2):
        numerators(1, h)
        direct[h] = [send(num.at[h, 1, 2:4], from_m.at[h, 2:4], a_next)]
    scale_rows(3)
    for h in range(2):
        numerators(3, h)
        direct[h].append(send(num.at[h, 3, 0:2], from_p.at[h, 0:2], a_last))

    for h in range(2):
        first_p[h].wait_recv()
        num[h, 1, 0:2] = num[h, 1, 0:2] + relay_p[h]
        second[h] = [send(num.at[h, 1, 0:2], from_m.at[h, 0:2], a_next)]
        first_m[h].wait_recv()
        num[h, 3, 2:4] = num[h, 3, 2:4] + relay_m[h]
        second[h].append(send(num.at[h, 3, 2:4], from_p.at[h, 2:4], a_last))

    mass = row_product(tgt_scale)
    outbox[9] = mass
    broadcast(9, plane_in.at[3], plane_peers, 12)

    scale_rows(0)
    for h in range(2):
        numerators(0, h)

    def gather(h):
        for copy in direct[h] + second[h]:
            copy.wait_recv()
        num[h, 0] = num[h, 0] + from_m[h] + from_p[h]

    half = OUT // 2
    up, down, over = (b + 1) % 4, (b + 3) % 4, (b + 2) % 4
    gather(0)
    far_p = send(num.at[0, 0, over, 0:half], relay2_p, b_next)
    far_m = send(num.at[0, 0, over, half:OUT], relay2_m, b_last)
    ends = [
        send(num.at[0, 0, up, half:OUT], from2_m.at[0, half:OUT], b_next),
        send(num.at[0, 0, down, 0:half], from2_p.at[0, 0:half], b_last),
    ]
    gather(1)
    ends.append(send(num.at[1, 0, over], over2, b_over))
    ends.append(send(num.at[1, 0, up], from2_m.at[1], b_next))
    ends.append(send(num.at[1, 0, down], from2_p.at[1], b_last))
    far_p.wait_recv()
    num[0, 0, up, 0:half] = num[0, 0, up, 0:half] + relay2_p[...]
    ends.append(send(num.at[0, 0, up, 0:half], from2_m.at[0, 0:half], b_next))
    far_m.wait_recv()
    num[0, 0, down, half:OUT] = num[0, 0, down, half:OUT] + relay2_m[...]
    ends.append(send(num.at[0, 0, down, half:OUT], from2_p.at[0, half:OUT], b_last))

    arrived(plane_in.at[3], 12)
    mass = mass + jnp.sum(plane_in[3], axis=0)
    logs = jnp.log(src_scale) + jnp.log(mass)
    sub = lax.broadcasted_iota(jnp.int32, (8, 128), 0)
    mine_now = sub == t // 2
    log_row = jnp.sum(jnp.where(mine_now, logs, 0.0), axis=0, keepdims=True)
    mass_row = jnp.sum(jnp.where(mine_now, mass, 0.0), axis=0, keepdims=True)
    odd = jnp.full((1, OUT), t % 2, jnp.int32) == 1
    log_ref[...] = jnp.where(odd, log_row[:, OUT:], log_row[:, :OUT])
    row_id = lax.broadcasted_iota(jnp.int32, (OUT, 128), 0) + (t % 2) * OUT
    lane_id = lax.broadcasted_iota(jnp.int32, (OUT, 128), 1)
    mass_col = jnp.sum(jnp.where(row_id == lane_id, mass_row, 0.0), axis=1, keepdims=True)

    for copy in ends:
        copy.wait_recv()
    final = num[0, 0, b] + from2_m[0] + from2_p[0]
    proj_ref[:, 0:WIDE] = (final / mass_col).astype(jnp.bfloat16)
    final = num[1, 0, b] + from2_m[1] + from2_p[1] + over2[...]
    proj_ref[:, WIDE:EMB] = (final / mass_col).astype(jnp.bfloat16)

    for i in range(ITERS):
        sent(plane_in.at[i], 4 * i)
        sent(far_in.at[i], 4 * i + 1)
        sent(near_in.at[i], 4 * i + 2)
        sent(core_in.at[i], 4 * i + 3)
    sent(plane_in.at[3], 12)
    for copy in started:
        copy.wait_send()


def body(n_z, source_cells, target_cells, source_mass, target_mass, source_order, tile_list, tile_count):
    vmem = pl.BlockSpec(memory_space=pltpu.VMEM)
    hbm = pl.BlockSpec(memory_space=pltpu.HBM)
    half = OUT // 2
    near = len([d for d in range(1, n_z) if min(d, n_z - d) < FAR])
    far = 2 * (n_z - 1 - near)
    f32, bf16, i32 = jnp.float32, jnp.bfloat16, jnp.int32
    projected, log_mass = pl.pallas_call(
        functools.partial(kernel, n_z),
        out_shape=(
            jax.ShapeDtypeStruct((OUT, EMB), bf16),
            jax.ShapeDtypeStruct((1, OUT), f32),
        ),
        in_specs=[hbm] * 6,
        out_specs=(vmem, vmem),
        scratch_shapes=[
            pltpu.VMEM((ROWS, EMB), bf16),
            pltpu.VMEM((COLS, EMB), bf16),
            pltpu.VMEM((8, 128), f32),
            pltpu.VMEM((8, 128), f32),
            pltpu.VMEM((1, ROWS), i32),
            pltpu.VMEM((1, SLOTS), i32),
            pltpu.VMEM((ROWS, EMB), bf16),
            pltpu.VMEM((COLS, EMB), bf16),
            pltpu.VMEM((ROWS, COLS), f32),
            pltpu.VMEM((ROWS, COLS), bf16),
            pltpu.VMEM((COLS, ROWS), bf16),
            pltpu.VMEM((BLK, COLS), bf16),
            pltpu.VMEM((10, 8, 128), f32),
            pltpu.VMEM((4, 15, 8, 128), f32),
            pltpu.VMEM((3, far, 8, 128), f32),
            pltpu.VMEM((3, near, 8, 128), f32),
            pltpu.VMEM((3, 1, 8, 128), f32),
            pltpu.VMEM((2, 4, 4, OUT, WIDE), f32),
            pltpu.VMEM((2, 2, OUT, WIDE), f32),
            pltpu.VMEM((2, 2, OUT, WIDE), f32),
            pltpu.VMEM((2, 4, OUT, WIDE), f32),
            pltpu.VMEM((2, 4, OUT, WIDE), f32),
            pltpu.VMEM((half, WIDE), f32),
            pltpu.VMEM((half, WIDE), f32),
            pltpu.VMEM((2, OUT, WIDE), f32),
            pltpu.VMEM((2, OUT, WIDE), f32),
            pltpu.VMEM((OUT, WIDE), f32),
            pltpu.SemaphoreType.DMA((6,)),
            pltpu.SemaphoreType.DMA((13,)),
            pltpu.SemaphoreType.DMA((13,)),
            pltpu.SemaphoreType.DMA((21,)),
            pltpu.SemaphoreType.DMA((21,)),
        ],
        compiler_params=pltpu.CompilerParams(
            collective_id=0, has_side_effects=True, vmem_limit_bytes=40 * 1024 * 1024
        ),
    )(
        *[
            pltpu.with_memory_space_constraint(operand, pltpu.HBM)
            for operand in (
                source_cells,
                target_cells,
                source_mass.reshape(8, 128),
                target_mass.reshape(8, 128),
                source_order.reshape(1, ROWS),
                tile_list,
            )
        ]
    )
    return projected, log_mass.reshape(OUT)


def solution(mesh):
    placed = (
        P("src", None),
        P("tgt", None),
        P("src"),
        P("tgt"),
        P("src"),
        P("src", "tgt"),
        P("src", "tgt"),
    )
    return jax.shard_map(
        functools.partial(body, mesh.shape["src"] // 2),
        mesh=mesh,
        in_specs=placed,
        out_specs=(P(("src", "tgt"), None), P(("src", "tgt"))),
        check_vma=False,
    )
```

```python
import functools

import jax
import jax.numpy as jnp
from jax import lax
from jax.experimental import pallas as pl
from jax.experimental.pallas import tpu as pltpu
from jax.sharding import PartitionSpec as P

EMB = 512
BLK = 256
ROWS = 1024
COLS = 1024
ITERS = 3
INVERSE_TEMP = 64.0
MASS_POWER = 0.8
NORM_EPSILON = 1e-06
SHARPNESS = INVERSE_TEMP / EMB
SLOTS = 12
OUT = 64
PARTS = 4
RELAYED = 2
WIDE = EMB // PARTS
FAR = 8
COPIES = 9 * PARTS + 3 * RELAYED
AHEAD = 2
MESH = pl.DeviceIdType.MESH


def normalize_into(cells, hat):
    def step(i, carry):
        rows = pl.ds(i * BLK, BLK)
        wide = cells[rows, :].astype(jnp.float32)
        mean = jnp.sum(wide * wide, axis=1, keepdims=True) * (1.0 / EMB)
        hat[rows, :] = (wide * lax.rsqrt(mean + NORM_EPSILON)).astype(jnp.bfloat16)
        return carry

    lax.fori_loop(0, ROWS // BLK, step, 0)


def power(x):
    return jnp.exp(MASS_POWER * jnp.log(x))


def as_row(tile):
    return jnp.concatenate([tile[k : k + 1, :] for k in range(8)], axis=1)


def split_rows(tile):
    which = lax.broadcasted_iota(jnp.int32, (8, 128), 0)
    pieces = []
    for k in range(8):
        value = jnp.broadcast_to(tile[k : k + 1, :], (8, 128))
        high = value.astype(jnp.bfloat16).astype(jnp.float32)
        piece = jnp.where(which == 0, high, jnp.where(which == 1, value - high, 0.0))
        pieces.append(piece.astype(jnp.bfloat16))
    return jnp.concatenate(pieces, axis=1)


def as_tile(rows):
    which = lax.broadcasted_iota(jnp.int32, (8, 128), 0)
    tile = jnp.zeros((8, 128), jnp.float32)
    for k in range(8):
        piece = jnp.sum(rows[:, k * 128 : (k + 1) * 128], axis=0, keepdims=True)
        tile = jnp.where(which == k, piece, tile)
    return tile


def kernel(
    n_z,
    src_hbm,
    tgt_hbm,
    smass_hbm,
    tmass_hbm,
    order_hbm,
    list_hbm,
    proj_ref,
    log_ref,
    src_ref,
    tgt_ref,
    smass_ref,
    tmass_ref,
    order_ref,
    list_ref,
    src_hat,
    tgt_hat,
    k_wide,
    k_half,
    k_turned,
    scaled,
    outbox,
    plane_in,
    far_in,
    near_in,
    core_in,
    num,
    relay_p,
    relay_m,
    from_m,
    from_p,
    relay2_p,
    relay2_m,
    from2_m,
    from2_p,
    over2,
    load_sem,
    small_send,
    small_recv,
    big_send,
    big_recv,
):
    s = lax.axis_index("src")
    t = lax.axis_index("tgt")
    z = s // 2
    core = s % 2
    y = t // 4
    x = t % 4

    plane_steps = [(dy, dx) for dy in range(4) for dx in range(4) if (dy, dx) != (0, 0)]
    plane_steps.sort(key=lambda d: -(min(d[0], 4 - d[0]) + min(d[1], 4 - d[1])))
    plane_peers = [(s, ((y + dy) % 4) * 4 + (x + dx) % 4) for dy, dx in plane_steps]
    z_steps = sorted(range(1, n_z), key=lambda d: -min(d, n_z - d))
    far_steps = [d for d in z_steps if min(d, n_z - d) >= FAR]
    near_steps = [d for d in z_steps if min(d, n_z - d) < FAR]
    far_peers = [
        (((z + d) % n_z) * 2 + side, t) for d in far_steps for side in (core, 1 - core)
    ]
    near_peers = [(((z + d) % n_z) * 2 + core, t) for d in near_steps]
    sibling = (z * 2 + 1 - core, t)

    def device(where):
        return {"src": where[0], "tgt": where[1]}

    barrier = pltpu.get_barrier_semaphore()
    everyone = far_peers + near_peers + plane_peers + [sibling]
    for where in everyone:
        pl.semaphore_signal(barrier, 1, device_id=device(where), device_id_type=MESH)
    loads = [
        pltpu.make_async_copy(there, here, load_sem.at[i])
        for i, (there, here) in enumerate(
            (
                (src_hbm, src_ref),
                (tgt_hbm, tgt_ref),
                (order_hbm, order_ref),
                (list_hbm, list_ref),
                (smass_hbm, smass_ref),
                (tmass_hbm, tmass_ref),
            )
        )
    ]
    for load in loads:
        load.start()
    loads[0].wait()
    normalize_into(src_ref, src_hat)
    loads[1].wait()
    normalize_into(tgt_ref, tgt_hat)
    for load in loads[2:]:
        load.wait()

    codes = jnp.maximum(list_ref[...], 0)
    live = list_ref[...] >= 0
    flags = jnp.where(live, jnp.int32(1) << codes, 0).astype(jnp.float32)
    bits = jnp.sum(flags, axis=1, keepdims=True).astype(jnp.int32)
    position = lax.broadcasted_iota(jnp.int32, (1, ROWS), 1)
    bits_row = jnp.broadcast_to(bits, (1, ROWS))
    nibble = (lax.shift_right_logical(bits_row, (position // BLK) * 4) & 15).astype(jnp.float32)

    def build(i, carry):
        rows = pl.ds(i * BLK, BLK)
        row_ids = lax.broadcasted_iota(jnp.int32, (BLK, 1), 0) + i * BLK
        placed = jnp.where(order_ref[...] == row_ids, nibble, 0.0)
        links = jnp.sum(placed, axis=1, keepdims=True).astype(jnp.int32)
        for q in range(COLS // BLK):
            cols = pl.ds(q * BLK, BLK)
            similarity = lax.dot_general(
                src_hat[rows, :],
                tgt_hat[cols, :],
                (((1,), (1,)), ((), ())),
                preferred_element_type=jnp.float32,
            )
            linked = (lax.shift_right_logical(links, q) & 1).astype(jnp.float32)
            tile = jnp.exp(similarity * SHARPNESS) * linked
            k_wide[rows, cols] = tile
            k_half[rows, cols] = tile.astype(jnp.bfloat16)
        return carry

    lax.fori_loop(0, ROWS // BLK, build, 0)

    def turn(i, carry):
        rows = pl.ds(i * BLK, BLK)
        for q in range(COLS // BLK):
            cols = pl.ds(q * BLK, BLK)
            k_turned[cols, rows] = jnp.transpose(k_wide[rows, cols]).astype(jnp.bfloat16)
        return carry

    def first_row_product(tile):
        return as_tile(
            lax.dot_general(
                split_rows(tile),
                k_half[...],
                (((1,), (1,)), ((), ())),
                preferred_element_type=jnp.float32,
            )
        )

    def row_product(tile):
        return as_tile(
            jnp.dot(split_rows(tile), k_turned[...], preferred_element_type=jnp.float32)
        )

    def col_product(tile):
        return as_tile(
            jnp.dot(split_rows(tile), k_half[...], preferred_element_type=jnp.float32)
        )

    def broadcast(box, inbox, peers, sem):
        for slot, where in enumerate(peers):
            pltpu.make_async_remote_copy(
                src_ref=outbox.at[box],
                dst_ref=inbox.at[slot],
                send_sem=small_send.at[sem],
                recv_sem=small_recv.at[sem],
                device_id=device(where),
                device_id_type=MESH,
            ).start()

    def arrived(inbox, sem):
        pltpu.make_async_copy(inbox, inbox, small_recv.at[sem]).wait()

    def sent(inbox, sem):
        pltpu.make_async_copy(inbox, inbox, small_send.at[sem]).wait()

    tgt_scale = jnp.ones((8, 128), jnp.float32)
    src_scale = jnp.ones((8, 128), jnp.float32)
    pl.semaphore_wait(barrier, len(everyone))
    for i in range(ITERS):
        mine = row_product(tgt_scale) if i else first_row_product(tgt_scale)
        outbox[3 * i] = mine
        broadcast(3 * i, plane_in.at[i], plane_peers, 4 * i)
        if i == 0:
            lax.fori_loop(0, ROWS // BLK, turn, 0)
        arrived(plane_in.at[i], 4 * i)
        src_scale = power(smass_ref[...] / (mine + jnp.sum(plane_in[i], axis=0)))

        mine = col_product(src_scale)
        outbox[3 * i + 1] = mine
        broadcast(3 * i + 1, far_in.at[i], far_peers, 4 * i + 1)
        broadcast(3 * i + 1, core_in.at[i], [sibling], 4 * i + 3)
        arrived(core_in.at[i], 4 * i + 3)
        mine = mine + core_in[i, 0]
        outbox[3 * i + 2] = mine
        broadcast(3 * i + 2, near_in.at[i], near_peers, 4 * i + 2)
        arrived(near_in.at[i], 4 * i + 2)
        mine = mine + jnp.sum(near_in[i], axis=0)
        arrived(far_in.at[i], 4 * i + 1)
        tgt_scale = power(tmass_ref[...] / (mine + jnp.sum(far_in[i], axis=0)))

    a = jnp.where(core == 0, x, y)
    b = jnp.where(core == 0, y, x)
    step_a = 1 + 3 * core
    step_b = 4 - 3 * core

    def at(a_now, b_now):
        return (s, (a_now % 4) * step_a + (b_now % 4) * step_b)

    tgt_row = as_row(tgt_scale)

    def scale_rows(d):
        for e in range(4):
            chunk = ((a + d) % 4) * step_a + e * step_b
            weighted = k_wide[pl.ds(chunk * OUT, OUT), :] * tgt_row
            scaled[e * OUT : (e + 1) * OUT, :] = weighted.astype(jnp.bfloat16)

    def numerators(d, first):
        wide = jnp.dot(
            scaled[...],
            tgt_ref[:, first * WIDE : first * WIDE + BLK],
            preferred_element_type=jnp.float32,
        )
        for h in range(first, first + BLK // WIDE):
            part = wide[:, (h - first) * WIDE : (h - first + 1) * WIDE]
            num[h, d] = part.reshape(4, OUT, WIDE)
        return range(first, first + BLK // WIDE)

    firsts = range(0, PARTS, BLK // WIDE)

    started = []

    def send(src, dst, where):
        sem = len(started)
        copy = pltpu.make_async_remote_copy(
            src_ref=src,
            dst_ref=dst,
            send_sem=big_send.at[sem],
            recv_sem=big_recv.at[sem],
            device_id=device(where),
            device_id_type=MESH,
        )
        copy.start()
        started.append(copy)
        return copy

    a_next, a_last = at(a + 1, b), at(a - 1, b)
    b_next, b_last, b_over = at(a, b + 1), at(a, b - 1), at(a, b + 2)
    first_p, first_m, direct, second = {}, {}, {}, {}
    scale_rows(2)
    for first in firsts:
        for h in numerators(2, first):
            first_p[h] = send(num.at[h, 2, 0:2], relay_p.at[h], a_next)
            first_m[h] = send(num.at[h, 2, 2:4], relay_m.at[h], a_last)
    scale_rows(1)
    for first in firsts:
        numerators(1, first)
    scale_rows(3)
    for first in firsts:
        numerators(3, first)
    direct[0] = [
        send(num.at[0, 1, 2:4], from_m.at[0, 2:4], a_next),
        send(num.at[0, 3, 0:2], from_p.at[0, 0:2], a_last),
    ]

    for h in range(PARTS):
        if h + 1 < PARTS:
            direct[h + 1] = [
                send(num.at[h + 1, 1, 2:4], from_m.at[h + 1, 2:4], a_next),
                send(num.at[h + 1, 3, 0:2], from_p.at[h + 1, 0:2], a_last),
            ]
        first_p[h].wait_recv()
        num[h, 1, 0:2] = num[h, 1, 0:2] + relay_p[h]
        second[h] = [send(num.at[h, 1, 0:2], from_m.at[h, 0:2], a_next)]
        first_m[h].wait_recv()
        num[h, 3, 2:4] = num[h, 3, 2:4] + relay_m[h]
        second[h].append(send(num.at[h, 3, 2:4], from_p.at[h, 2:4], a_last))

    mass = row_product(tgt_scale)
    outbox[9] = mass
    broadcast(9, plane_in.at[3], plane_peers, 12)

    scale_rows(0)
    for first in firsts:
        numerators(0, first)

    def gather(h):
        for copy in direct[h] + second[h]:
            copy.wait_recv()
        num[h, 0] = num[h, 0] + from_m[h] + from_p[h]

    half = OUT // 2
    up, down, over = (b + 1) % 4, (b + 3) % 4, (b + 2) % 4
    far_p, far_m = {}, {}
    ends = {h: [] for h in range(PARTS)}

    def pass_on(h):
        far_p[h].wait_recv()
        num[h, 0, up, 0:half] = num[h, 0, up, 0:half] + relay2_p[h]
        ends[h].append(send(num.at[h, 0, up, 0:half], from2_m.at[h, 0:half], b_next))
        far_m[h].wait_recv()
        num[h, 0, down, half:OUT] = num[h, 0, down, half:OUT] + relay2_m[h]
        ends[h].append(send(num.at[h, 0, down, half:OUT], from2_p.at[h, half:OUT], b_last))

    for h in range(PARTS):
        gather(h)
        if h < RELAYED:
            far_p[h] = send(num.at[h, 0, over, 0:half], relay2_p.at[h], b_next)
            far_m[h] = send(num.at[h, 0, over, half:OUT], relay2_m.at[h], b_last)
            ends[h].append(send(num.at[h, 0, up, half:OUT], from2_m.at[h, half:OUT], b_next))
            ends[h].append(send(num.at[h, 0, down, 0:half], from2_p.at[h, 0:half], b_last))
        else:
            ends[h].append(send(num.at[h, 0, over], over2.at[h - RELAYED], b_over))
            ends[h].append(send(num.at[h, 0, up], from2_m.at[h], b_next))
            ends[h].append(send(num.at[h, 0, down], from2_p.at[h], b_last))
        if h >= AHEAD and h - AHEAD < RELAYED:
            pass_on(h - AHEAD)
    for h in range(max(PARTS - AHEAD, 0), RELAYED):
        pass_on(h)

    arrived(plane_in.at[3], 12)
    mass = mass + jnp.sum(plane_in[3], axis=0)
    logs = jnp.log(src_scale) + jnp.log(mass)
    sub = lax.broadcasted_iota(jnp.int32, (8, 128), 0)
    mine_now = sub == t // 2
    log_row = jnp.sum(jnp.where(mine_now, logs, 0.0), axis=0, keepdims=True)
    mass_row = jnp.sum(jnp.where(mine_now, mass, 0.0), axis=0, keepdims=True)
    odd = jnp.full((1, OUT), t % 2, jnp.int32) == 1
    log_ref[...] = jnp.where(odd, log_row[:, OUT:], log_row[:, :OUT])
    row_id = lax.broadcasted_iota(jnp.int32, (OUT, 128), 0) + (t % 2) * OUT
    lane_id = lax.broadcasted_iota(jnp.int32, (OUT, 128), 1)
    mass_col = jnp.sum(jnp.where(row_id == lane_id, mass_row, 0.0), axis=1, keepdims=True)

    for i in range(ITERS):
        sent(plane_in.at[i], 4 * i)
        sent(far_in.at[i], 4 * i + 1)
        sent(near_in.at[i], 4 * i + 2)
        sent(core_in.at[i], 4 * i + 3)
    sent(plane_in.at[3], 12)
    for copy in started:
        copy.wait_send()

    for h in range(PARTS):
        for copy in ends[h]:
            copy.wait_recv()
        final = num[h, 0, b] + from2_m[h] + from2_p[h]
        if h >= RELAYED:
            final = final + over2[h - RELAYED]
        proj_ref[:, h * WIDE : (h + 1) * WIDE] = (final / mass_col).astype(jnp.bfloat16)


def hand_out(projected, log_mass, projected_out, log_out):
    projected_out[...] = projected[...]
    log_out[...] = log_mass[...]


def body(n_z, source_cells, target_cells, source_mass, target_mass, source_order, tile_list, tile_count):
    vmem = pl.BlockSpec(memory_space=pltpu.VMEM)
    hbm = pl.BlockSpec(memory_space=pltpu.HBM)
    half = OUT // 2
    near = len([d for d in range(1, n_z) if min(d, n_z - d) < FAR])
    far = 2 * (n_z - 1 - near)
    f32, bf16, i32 = jnp.float32, jnp.bfloat16, jnp.int32
    projected, log_mass = pl.pallas_call(
        functools.partial(kernel, n_z),
        out_shape=(
            jax.ShapeDtypeStruct((OUT, EMB), bf16),
            jax.ShapeDtypeStruct((1, OUT), f32),
        ),
        in_specs=[hbm] * 6,
        out_specs=(vmem, vmem),
        scratch_shapes=[
            pltpu.VMEM((ROWS, EMB), bf16),
            pltpu.VMEM((COLS, EMB), bf16),
            pltpu.VMEM((8, 128), f32),
            pltpu.VMEM((8, 128), f32),
            pltpu.VMEM((1, ROWS), i32),
            pltpu.VMEM((1, SLOTS), i32),
            pltpu.VMEM((ROWS, EMB), bf16),
            pltpu.VMEM((COLS, EMB), bf16),
            pltpu.VMEM((ROWS, COLS), f32),
            pltpu.VMEM((ROWS, COLS), bf16),
            pltpu.VMEM((COLS, ROWS), bf16),
            pltpu.VMEM((BLK, COLS), bf16),
            pltpu.VMEM((10, 8, 128), f32),
            pltpu.VMEM((4, 15, 8, 128), f32),
            pltpu.VMEM((3, far, 8, 128), f32),
            pltpu.VMEM((3, near, 8, 128), f32),
            pltpu.VMEM((3, 1, 8, 128), f32),
            pltpu.VMEM((PARTS, 4, 4, OUT, WIDE), f32),
            pltpu.VMEM((PARTS, 2, OUT, WIDE), f32),
            pltpu.VMEM((PARTS, 2, OUT, WIDE), f32),
            pltpu.VMEM((PARTS, 4, OUT, WIDE), f32),
            pltpu.VMEM((PARTS, 4, OUT, WIDE), f32),
            pltpu.VMEM((RELAYED, half, WIDE), f32),
            pltpu.VMEM((RELAYED, half, WIDE), f32),
            pltpu.VMEM((PARTS, OUT, WIDE), f32),
            pltpu.VMEM((PARTS, OUT, WIDE), f32),
            pltpu.VMEM((PARTS - RELAYED, OUT, WIDE), f32),
            pltpu.SemaphoreType.DMA((6,)),
            pltpu.SemaphoreType.DMA((13,)),
            pltpu.SemaphoreType.DMA((13,)),
            pltpu.SemaphoreType.DMA((COPIES,)),
            pltpu.SemaphoreType.DMA((COPIES,)),
        ],
        compiler_params=pltpu.CompilerParams(
            collective_id=0, has_side_effects=True, vmem_limit_bytes=40 * 1024 * 1024
        ),
    )(
        *[
            pltpu.with_memory_space_constraint(operand, pltpu.HBM)
            for operand in (
                source_cells,
                target_cells,
                source_mass.reshape(8, 128),
                target_mass.reshape(8, 128),
                source_order.reshape(1, ROWS),
                tile_list,
            )
        ]
    )
    projected, log_mass = pl.pallas_call(
        hand_out,
        out_shape=(
            jax.ShapeDtypeStruct((OUT, EMB), bf16),
            jax.ShapeDtypeStruct((1, OUT), f32),
        ),
        in_specs=[vmem] * 2,
        out_specs=(vmem, vmem),
    )(
        pltpu.with_memory_space_constraint(projected, pltpu.VMEM),
        pltpu.with_memory_space_constraint(log_mass, pltpu.VMEM),
    )
    return projected, log_mass.reshape(OUT)


def solution(mesh):
    placed = (
        P("src", None),
        P("tgt", None),
        P("src"),
        P("tgt"),
        P("src"),
        P("src", "tgt"),
        P("src", "tgt"),
    )
    return jax.shard_map(
        functools.partial(body, mesh.shape["src"] // 2),
        mesh=mesh,
        in_specs=placed,
        out_specs=(P(("src", "tgt"), None), P(("src", "tgt"))),
        check_vma=False,
    )
```

```python
import functools

import jax
import jax.numpy as jnp
from jax import lax
from jax.experimental import pallas as pl
from jax.experimental.pallas import tpu as pltpu
from jax.sharding import PartitionSpec as P

EMB = 512
BLK = 256
ROWS = 1024
COLS = 1024
ITERS = 3
INVERSE_TEMP = 64.0
MASS_POWER = 0.8
NORM_EPSILON = 1e-06
SHARPNESS = INVERSE_TEMP / EMB
SLOTS = 12
OUT = 64
PARTS = 4
RELAYED = 2
WIDE = EMB // PARTS
FAR = 8
COPIES = 9 * PARTS + 3 * RELAYED
AHEAD = 2
MESH = pl.DeviceIdType.MESH


def normalize_into(cells, hat):
    def step(i, carry):
        rows = pl.ds(i * BLK, BLK)
        wide = cells[rows, :].astype(jnp.float32)
        mean = jnp.sum(wide * wide, axis=1, keepdims=True) * (1.0 / EMB)
        hat[rows, :] = (wide * lax.rsqrt(mean + NORM_EPSILON)).astype(jnp.bfloat16)
        return carry

    lax.fori_loop(0, ROWS // BLK, step, 0, unroll=True)


def power(x):
    return jnp.exp(MASS_POWER * jnp.log(x))


def as_row(tile):
    return jnp.concatenate([tile[k : k + 1, :] for k in range(8)], axis=1)


def split_rows(tile):
    which = lax.broadcasted_iota(jnp.int32, (8, 128), 0)
    pieces = []
    for k in range(8):
        value = jnp.broadcast_to(tile[k : k + 1, :], (8, 128))
        high = value.astype(jnp.bfloat16).astype(jnp.float32)
        piece = jnp.where(which == 0, high, jnp.where(which == 1, value - high, 0.0))
        pieces.append(piece.astype(jnp.bfloat16))
    return jnp.concatenate(pieces, axis=1)


def as_tile(rows):
    which = lax.broadcasted_iota(jnp.int32, (8, 128), 0)
    tile = jnp.zeros((8, 128), jnp.float32)
    for k in range(8):
        piece = jnp.sum(rows[:, k * 128 : (k + 1) * 128], axis=0, keepdims=True)
        tile = jnp.where(which == k, piece, tile)
    return tile


def kernel(
    n_z,
    src_hbm,
    tgt_hbm,
    smass_hbm,
    tmass_hbm,
    order_hbm,
    list_hbm,
    proj_ref,
    log_ref,
    src_ref,
    tgt_ref,
    smass_ref,
    tmass_ref,
    order_ref,
    list_ref,
    src_hat,
    tgt_hat,
    links,
    k_wide,
    k_half,
    k_turned,
    scaled,
    outbox,
    plane_in,
    far_in,
    near_in,
    core_in,
    num,
    relay_p,
    relay_m,
    from_m,
    from_p,
    relay2_p,
    relay2_m,
    from2_m,
    from2_p,
    over2,
    passed_on,
    load_sem,
    small_send,
    small_recv,
    big_send,
    big_recv,
):
    s = lax.axis_index("src")
    t = lax.axis_index("tgt")
    z = s // 2
    core = s % 2
    y = t // 4
    x = t % 4

    plane_steps = [(dy, dx) for dy in range(4) for dx in range(4) if (dy, dx) != (0, 0)]
    plane_steps.sort(key=lambda d: -(min(d[0], 4 - d[0]) + min(d[1], 4 - d[1])))
    plane_peers = [(s, ((y + dy) % 4) * 4 + (x + dx) % 4) for dy, dx in plane_steps]
    z_steps = sorted(range(1, n_z), key=lambda d: -min(d, n_z - d))
    far_steps = [d for d in z_steps if min(d, n_z - d) >= FAR]
    near_steps = [d for d in z_steps if min(d, n_z - d) < FAR]
    far_peers = [
        (((z + d) % n_z) * 2 + side, t) for d in far_steps for side in (core, 1 - core)
    ]
    near_peers = [(((z + d) % n_z) * 2 + core, t) for d in near_steps]
    sibling = (z * 2 + 1 - core, t)

    def device(where):
        return {"src": where[0], "tgt": where[1]}

    loads = {}

    def load(name, there, here):
        loads[name] = pltpu.make_async_copy(there, here, load_sem.at[len(loads)])
        loads[name].start()

    load("order", order_hbm, order_ref)
    load("list", list_hbm, list_ref)
    for i in range(ROWS // BLK):
        rows = pl.ds(i * BLK, BLK)
        load(("tgt", i), tgt_hbm.at[rows], tgt_ref.at[rows])
        load(("src", i), src_hbm.at[rows], src_ref.at[rows])
    load("smass", smass_hbm, smass_ref)
    load("tmass", tmass_hbm, tmass_ref)

    barrier = pltpu.get_barrier_semaphore()
    reach = n_z // 4
    relays = [((z + d) % n_z * 2 + core, t) for d in (reach, n_z - reach)]
    greeted = [((z + d) % n_z * 2 + 1 - core, t) for d in (reach, n_z - reach)]
    greeted += [((z + d) % n_z * 2 + core, t) for d in z_steps if min(d, n_z - d) <= reach]
    greeted += plane_peers + [sibling]
    for where in greeted:
        pl.semaphore_signal(barrier, 1, device_id=device(where), device_id_type=MESH)
    loads["order"].wait()
    loads["list"].wait()
    codes = jnp.maximum(list_ref[...], 0)
    live = list_ref[...] >= 0
    flags = jnp.where(live, jnp.int32(1) << codes, 0).astype(jnp.float32)
    bits = jnp.sum(flags, axis=1, keepdims=True).astype(jnp.int32)
    position = lax.broadcasted_iota(jnp.int32, (1, ROWS), 1)
    bits_row = jnp.broadcast_to(bits, (1, ROWS))
    nibble = (lax.shift_right_logical(bits_row, (position // BLK) * 4) & 15).astype(jnp.float32)

    def find_links(i, carry):
        row_ids = lax.broadcasted_iota(jnp.int32, (BLK, 1), 0) + i * BLK
        placed = jnp.where(order_ref[...] == row_ids, nibble, 0.0)
        links[pl.ds(i * BLK, BLK), :] = jnp.sum(placed, axis=1, keepdims=True)
        return carry

    lax.fori_loop(0, ROWS // BLK, find_links, 0, unroll=True)

    for i in range(ROWS // BLK):
        loads["tgt", i].wait()
    normalize_into(tgt_ref, tgt_hat)
    for i in range(ROWS // BLK):
        loads["src", i].wait()
    normalize_into(src_ref, src_hat)
    loads["smass"].wait()
    loads["tmass"].wait()

    def build(i, carry):
        rows = pl.ds(i * BLK, BLK)
        linked_to = links[rows, :].astype(jnp.int32)
        for q in range(COLS // BLK):
            cols = pl.ds(q * BLK, BLK)
            similarity = lax.dot_general(
                src_hat[rows, :],
                tgt_hat[cols, :],
                (((1,), (1,)), ((), ())),
                preferred_element_type=jnp.float32,
            )
            linked = (lax.shift_right_logical(linked_to, q) & 1).astype(jnp.float32)
            tile = jnp.exp(similarity * SHARPNESS) * linked
            k_wide[rows, cols] = tile
            k_half[rows, cols] = tile.astype(jnp.bfloat16)
        return carry

    lax.fori_loop(0, ROWS // BLK, build, 0, unroll=True)

    def turn(i, carry):
        rows = pl.ds(i * BLK, BLK)
        for q in range(COLS // BLK):
            cols = pl.ds(q * BLK, BLK)
            k_turned[cols, rows] = jnp.transpose(k_wide[rows, cols]).astype(jnp.bfloat16)
        return carry

    def first_row_product(tile):
        return as_tile(
            lax.dot_general(
                split_rows(tile),
                k_half[...],
                (((1,), (1,)), ((), ())),
                preferred_element_type=jnp.float32,
            )
        )

    def row_product(tile):
        return as_tile(
            jnp.dot(split_rows(tile), k_turned[...], preferred_element_type=jnp.float32)
        )

    def col_product(tile):
        return as_tile(
            jnp.dot(split_rows(tile), k_half[...], preferred_element_type=jnp.float32)
        )

    def broadcast(box, inbox, peers, sem):
        for slot, where in enumerate(peers):
            pltpu.make_async_remote_copy(
                src_ref=outbox.at[box],
                dst_ref=inbox.at[slot],
                send_sem=small_send.at[sem],
                recv_sem=small_recv.at[sem],
                device_id=device(where),
                device_id_type=MESH,
            ).start()

    def arrived(inbox, sem):
        pltpu.make_async_copy(inbox, inbox, small_recv.at[sem]).wait()

    def sent(inbox, sem):
        pltpu.make_async_copy(inbox, inbox, small_send.at[sem]).wait()

    tgt_scale = jnp.ones((8, 128), jnp.float32)
    src_scale = jnp.ones((8, 128), jnp.float32)
    pl.semaphore_wait(barrier, len(greeted))
    for where in relays:
        pl.semaphore_signal(passed_on, 1, device_id=device(where), device_id_type=MESH)
    for i in range(ITERS):
        mine = row_product(tgt_scale) if i else first_row_product(tgt_scale)
        outbox[3 * i] = mine
        broadcast(3 * i, plane_in.at[i], plane_peers, 4 * i)
        if i == 0:
            lax.fori_loop(0, ROWS // BLK, turn, 0)
        arrived(plane_in.at[i], 4 * i)
        src_scale = power(smass_ref[...] / (mine + jnp.sum(plane_in[i], axis=0)))

        mine = col_product(src_scale)
        outbox[3 * i + 1] = mine
        if i == 0:
            pl.semaphore_wait(passed_on, len(relays))
        broadcast(3 * i + 1, far_in.at[i], far_peers, 4 * i + 1)
        broadcast(3 * i + 1, core_in.at[i], [sibling], 4 * i + 3)
        arrived(core_in.at[i], 4 * i + 3)
        mine = mine + core_in[i, 0]
        outbox[3 * i + 2] = mine
        broadcast(3 * i + 2, near_in.at[i], near_peers, 4 * i + 2)
        arrived(near_in.at[i], 4 * i + 2)
        mine = mine + jnp.sum(near_in[i], axis=0)
        arrived(far_in.at[i], 4 * i + 1)
        tgt_scale = power(tmass_ref[...] / (mine + jnp.sum(far_in[i], axis=0)))

    a = jnp.where(core == 0, x, y)
    b = jnp.where(core == 0, y, x)
    step_a = 1 + 3 * core
    step_b = 4 - 3 * core

    def at(a_now, b_now):
        return (s, (a_now % 4) * step_a + (b_now % 4) * step_b)

    tgt_row = as_row(tgt_scale)

    def scale_rows(d):
        for e in range(4):
            chunk = ((a + d) % 4) * step_a + e * step_b
            weighted = k_wide[pl.ds(chunk * OUT, OUT), :] * tgt_row
            scaled[e * OUT : (e + 1) * OUT, :] = weighted.astype(jnp.bfloat16)

    def numerators(d, first):
        wide = jnp.dot(
            scaled[...],
            tgt_ref[:, first * WIDE : first * WIDE + BLK],
            preferred_element_type=jnp.float32,
        )
        for h in range(first, first + BLK // WIDE):
            part = wide[:, (h - first) * WIDE : (h - first + 1) * WIDE]
            num[h, d] = part.reshape(4, OUT, WIDE)
        return range(first, first + BLK // WIDE)

    firsts = range(0, PARTS, BLK // WIDE)

    started = []

    def send(src, dst, where):
        sem = len(started)
        copy = pltpu.make_async_remote_copy(
            src_ref=src,
            dst_ref=dst,
            send_sem=big_send.at[sem],
            recv_sem=big_recv.at[sem],
            device_id=device(where),
            device_id_type=MESH,
        )
        copy.start()
        started.append(copy)
        return copy

    a_next, a_last = at(a + 1, b), at(a - 1, b)
    b_next, b_last, b_over = at(a, b + 1), at(a, b - 1), at(a, b + 2)
    first_p, first_m, direct, second = {}, {}, {}, {}
    scale_rows(2)
    for first in firsts:
        for h in numerators(2, first):
            first_p[h] = send(num.at[h, 2, 0:2], relay_p.at[h], a_next)
            first_m[h] = send(num.at[h, 2, 2:4], relay_m.at[h], a_last)
    scale_rows(1)
    for first in firsts:
        numerators(1, first)
    scale_rows(3)
    for first in firsts:
        numerators(3, first)
    direct[0] = [
        send(num.at[0, 1, 2:4], from_m.at[0, 2:4], a_next),
        send(num.at[0, 3, 0:2], from_p.at[0, 0:2], a_last),
    ]

    for h in range(PARTS):
        if h + 1 < PARTS:
            direct[h + 1] = [
                send(num.at[h + 1, 1, 2:4], from_m.at[h + 1, 2:4], a_next),
                send(num.at[h + 1, 3, 0:2], from_p.at[h + 1, 0:2], a_last),
            ]
        first_p[h].wait_recv()
        num[h, 1, 0:2] = num[h, 1, 0:2] + relay_p[h]
        second[h] = [send(num.at[h, 1, 0:2], from_m.at[h, 0:2], a_next)]
        first_m[h].wait_recv()
        num[h, 3, 2:4] = num[h, 3, 2:4] + relay_m[h]
        second[h].append(send(num.at[h, 3, 2:4], from_p.at[h, 2:4], a_last))

    mass = row_product(tgt_scale)
    outbox[9] = mass
    broadcast(9, plane_in.at[3], plane_peers, 12)

    scale_rows(0)
    for first in firsts:
        numerators(0, first)

    def gather(h):
        for copy in direct[h] + second[h]:
            copy.wait_recv()
        num[h, 0] = num[h, 0] + from_m[h] + from_p[h]

    half = OUT // 2
    up, down, over = (b + 1) % 4, (b + 3) % 4, (b + 2) % 4
    far_p, far_m = {}, {}
    ends = {h: [] for h in range(PARTS)}

    def pass_on(h):
        far_p[h].wait_recv()
        num[h, 0, up, 0:half] = num[h, 0, up, 0:half] + relay2_p[h]
        ends[h].append(send(num.at[h, 0, up, 0:half], from2_m.at[h, 0:half], b_next))
        far_m[h].wait_recv()
        num[h, 0, down, half:OUT] = num[h, 0, down, half:OUT] + relay2_m[h]
        ends[h].append(send(num.at[h, 0, down, half:OUT], from2_p.at[h, half:OUT], b_last))

    for h in range(PARTS):
        gather(h)
        if h < RELAYED:
            far_p[h] = send(num.at[h, 0, over, 0:half], relay2_p.at[h], b_next)
            far_m[h] = send(num.at[h, 0, over, half:OUT], relay2_m.at[h], b_last)
            ends[h].append(send(num.at[h, 0, up, half:OUT], from2_m.at[h, half:OUT], b_next))
            ends[h].append(send(num.at[h, 0, down, 0:half], from2_p.at[h, 0:half], b_last))
        else:
            ends[h].append(send(num.at[h, 0, over], over2.at[h - RELAYED], b_over))
            ends[h].append(send(num.at[h, 0, up], from2_m.at[h], b_next))
            ends[h].append(send(num.at[h, 0, down], from2_p.at[h], b_last))
        if h >= AHEAD and h - AHEAD < RELAYED:
            pass_on(h - AHEAD)
    for h in range(max(PARTS - AHEAD, 0), RELAYED):
        pass_on(h)

    arrived(plane_in.at[3], 12)
    mass = mass + jnp.sum(plane_in[3], axis=0)
    logs = jnp.log(src_scale) + jnp.log(mass)
    sub = lax.broadcasted_iota(jnp.int32, (8, 128), 0)
    mine_now = sub == t // 2
    log_row = jnp.sum(jnp.where(mine_now, logs, 0.0), axis=0, keepdims=True)
    mass_row = jnp.sum(jnp.where(mine_now, mass, 0.0), axis=0, keepdims=True)
    odd = jnp.full((1, OUT), t % 2, jnp.int32) == 1
    log_ref[...] = jnp.where(odd, log_row[:, OUT:], log_row[:, :OUT])
    row_id = lax.broadcasted_iota(jnp.int32, (OUT, 128), 0) + (t % 2) * OUT
    lane_id = lax.broadcasted_iota(jnp.int32, (OUT, 128), 1)
    mass_col = jnp.sum(jnp.where(row_id == lane_id, mass_row, 0.0), axis=1, keepdims=True)

    for i in range(ITERS):
        sent(plane_in.at[i], 4 * i)
        sent(far_in.at[i], 4 * i + 1)
        sent(near_in.at[i], 4 * i + 2)
        sent(core_in.at[i], 4 * i + 3)
    sent(plane_in.at[3], 12)
    for copy in started:
        copy.wait_send()

    for h in range(PARTS):
        for copy in ends[h]:
            copy.wait_recv()
        final = num[h, 0, b] + from2_m[h] + from2_p[h]
        if h >= RELAYED:
            final = final + over2[h - RELAYED]
        proj_ref[:, h * WIDE : (h + 1) * WIDE] = (final / mass_col).astype(jnp.bfloat16)


def hand_out(projected, log_mass, projected_out, log_out):
    projected_out[...] = projected[...]
    log_out[...] = log_mass[...]


def body(n_z, source_cells, target_cells, source_mass, target_mass, source_order, tile_list, tile_count):
    vmem = pl.BlockSpec(memory_space=pltpu.VMEM)
    hbm = pl.BlockSpec(memory_space=pltpu.HBM)
    half = OUT // 2
    near = len([d for d in range(1, n_z) if min(d, n_z - d) < FAR])
    far = 2 * (n_z - 1 - near)
    f32, bf16, i32 = jnp.float32, jnp.bfloat16, jnp.int32
    projected, log_mass = pl.pallas_call(
        functools.partial(kernel, n_z),
        out_shape=(
            jax.ShapeDtypeStruct((OUT, EMB), bf16),
            jax.ShapeDtypeStruct((1, OUT), f32),
        ),
        in_specs=[hbm] * 6,
        out_specs=(vmem, vmem),
        scratch_shapes=[
            pltpu.VMEM((ROWS, EMB), bf16),
            pltpu.VMEM((COLS, EMB), bf16),
            pltpu.VMEM((8, 128), f32),
            pltpu.VMEM((8, 128), f32),
            pltpu.VMEM((1, ROWS), i32),
            pltpu.VMEM((1, SLOTS), i32),
            pltpu.VMEM((ROWS, EMB), bf16),
            pltpu.VMEM((COLS, EMB), bf16),
            pltpu.VMEM((ROWS, 1), f32),
            pltpu.VMEM((ROWS, COLS), f32),
            pltpu.VMEM((ROWS, COLS), bf16),
            pltpu.VMEM((COLS, ROWS), bf16),
            pltpu.VMEM((BLK, COLS), bf16),
            pltpu.VMEM((10, 8, 128), f32),
            pltpu.VMEM((4, 15, 8, 128), f32),
            pltpu.VMEM((3, far, 8, 128), f32),
            pltpu.VMEM((3, near, 8, 128), f32),
            pltpu.VMEM((3, 1, 8, 128), f32),
            pltpu.VMEM((PARTS, 4, 4, OUT, WIDE), f32),
            pltpu.VMEM((PARTS, 2, OUT, WIDE), f32),
            pltpu.VMEM((PARTS, 2, OUT, WIDE), f32),
            pltpu.VMEM((PARTS, 4, OUT, WIDE), f32),
            pltpu.VMEM((PARTS, 4, OUT, WIDE), f32),
            pltpu.VMEM((RELAYED, half, WIDE), f32),
            pltpu.VMEM((RELAYED, half, WIDE), f32),
            pltpu.VMEM((PARTS, OUT, WIDE), f32),
            pltpu.VMEM((PARTS, OUT, WIDE), f32),
            pltpu.VMEM((PARTS - RELAYED, OUT, WIDE), f32),
            pltpu.SemaphoreType.REGULAR,
            pltpu.SemaphoreType.DMA((12,)),
            pltpu.SemaphoreType.DMA((13,)),
            pltpu.SemaphoreType.DMA((13,)),
            pltpu.SemaphoreType.DMA((COPIES,)),
            pltpu.SemaphoreType.DMA((COPIES,)),
        ],
        compiler_params=pltpu.CompilerParams(
            collective_id=0, has_side_effects=True, vmem_limit_bytes=40 * 1024 * 1024
        ),
    )(
        *[
            pltpu.with_memory_space_constraint(operand, pltpu.HBM)
            for operand in (
                source_cells,
                target_cells,
                source_mass.reshape(8, 128),
                target_mass.reshape(8, 128),
                source_order.reshape(1, ROWS),
                tile_list,
            )
        ]
    )
    projected, log_mass = pl.pallas_call(
        hand_out,
        out_shape=(
            jax.ShapeDtypeStruct((OUT, EMB), bf16),
            jax.ShapeDtypeStruct((1, OUT), f32),
        ),
        in_specs=[vmem] * 2,
        out_specs=(vmem, vmem),
    )(
        pltpu.with_memory_space_constraint(projected, pltpu.VMEM),
        pltpu.with_memory_space_constraint(log_mass, pltpu.VMEM),
    )
    return projected, log_mass.reshape(OUT)


def solution(mesh):
    placed = (
        P("src", None),
        P("tgt", None),
        P("src"),
        P("tgt"),
        P("src"),
        P("src", "tgt"),
        P("src", "tgt"),
    )
    return jax.shard_map(
        functools.partial(body, mesh.shape["src"] // 2),
        mesh=mesh,
        in_specs=placed,
        out_specs=(P(("src", "tgt"), None), P(("src", "tgt"))),
        check_vma=False,
    )
```
